32 devices in a mesh: dp: 2 (over x), expert: 16 (over z, y, core).
Axes of the slice: x: 2, y: 2, z: 4, core: 2. Of those that a mesh axis runs over, the one named last changes fastest.
Arguments:
- tokens: bfloat16 [16, 1024, 2048], P('expert', 'dp'), may hold values from -6 to 6
- segments: int32 [16, 1024], P('expert'), may hold values from 0 to 3, never falling along the last dimension, each value on 1 to 512 neighbouring positions
- routes: int32 [16, 1024, 6], P('expert', 'dp'), may hold values from 0 to 15, all different within a row; in each aligned block of 512 rows (0 to 511, 512 to 1023, ..., all dimensions but the last counted through in order) at most 256 rows name the same one
- combine: float32 [16, 1024, 6], P('expert', 'dp'), may hold values from 0.05 to 0.4
- input_gain: bfloat16 [2048], P(('dp', 'expert')), may hold values from 0.099609375 to 1.8984375
- query_weight: bfloat16 [2048, 3072], P(('dp', 'expert')), may hold values from -0.125 to 0.125
- latent_weight: bfloat16 [2048, 576], P(('dp', 'expert')), may hold values from -0.125 to 0.125
- latent_gain: bfloat16 [512], P(('dp', 'expert')), may hold values from 0.099609375 to 1.8984375
- expand_weight: bfloat16 [512, 4096], P(None, ('dp', 'expert')), may hold values from -0.25 to 0.25
- output_weight: bfloat16 [2048, 2048], P(None, ('dp', 'expert')), may hold values from -1 to 1
- middle_gain: bfloat16 [2048], P(('dp', 'expert')), may hold values from 0.099609375 to 1.8984375
- shared_gate: bfloat16 [2048, 2816], P(('dp', 'expert')), may hold values from -0.125 to 0.125
- shared_up: bfloat16 [2048, 2816], P(('dp', 'expert')), may hold values from -0.125 to 0.125
- shared_down: bfloat16 [2816, 2048], P(None, ('dp', 'expert')), may hold values from -0.109375 to 0.109375
- expert_gate: bfloat16 [16, 2048, 1408], P('expert', 'dp'), may hold values from -0.125 to 0.125
- expert_up: bfloat16 [16, 2048, 1408], P('expert', 'dp'), may hold values from -0.125 to 0.125
- expert_down: bfloat16 [16, 1408, 2048], P('expert', None, 'dp'), may hold values from -0.15625 to 0.15625
- cotangent: bfloat16 [16, 1024, 2048], P('expert', 'dp'), may hold values from -6 to 6
Outputs:
- output: bfloat16 [16, 1024, 2048], P('expert', 'dp')
- input_grad: float32 [16, 1024, 2048], P('expert', 'dp')
- input_gain_grad: float32 [2048], P(('dp', 'expert'))
- query_weight_grad: float32 [2048, 3072], P(('dp', 'expert'))
- latent_weight_grad: float32 [2048, 576], P(('dp', 'expert'))
- latent_gain_grad: float32 [512], P(('dp', 'expert'))
- expand_weight_grad: float32 [512, 4096], P(None, ('dp', 'expert'))
- output_weight_grad: float32 [2048, 2048], P(None, ('dp', 'expert'))
- middle_gain_grad: float32 [2048], P(('dp', 'expert'))
- shared_gate_grad: float32 [2048, 2816], P(('dp', 'expert'))
- shared_up_grad: float32 [2048, 2816], P(('dp', 'expert'))
- shared_down_grad: float32 [2816, 2048], P(None, ('dp', 'expert'))
- expert_gate_grad: float32 [16, 2048, 1408], P('expert', 'dp')
- expert_up_grad: float32 [16, 2048, 1408], P('expert', 'dp')
- expert_down_grad: float32 [16, 1408, 2048], P('expert', None, 'dp')
The draws below stay inside these ranges and needn't reach their ends.
Inputs may be any that keep to these rules, and one draw needn't show every extreme that they name: `segments`: numbers never fall along a sequence; equal numbers mark one document of at most 512 positions. `routes`: the 6 entries of a token name different experts; in each aligned block of 512 positions of a sequence no expert is named by more than 256 tokens, and some block reaches 256.
All inputs are finite; a program needn't handle non-finite values.
Results may differ from the reference program's by a relative error of at most 0.02.
Values may be sent and summed in bfloat16 or wider, within the bound.
A program may use at most 512 MiB of HBM per device.

```python
import math
import jax
import jax.numpy as jnp
import numpy as np
from jax import lax

D = 2048
HEADS = 16
NOPE = 128
ROPE = 64
VDIM = 128
RANK = 512
FE = 1408
FS = 2816
TOP = 6
EXPERTS = 16
SEQ = 1024
NSEQ = 16
TDS = 512
CAPS = 256


def block_scale(own_key, dims, cuts, low, largest):
    level, own = 1.0, jax.random.fold_in(own_key, 6)
    for axis_at, shards_of in cuts:
        heights = jnp.exp(jax.random.uniform(jax.random.fold_in(own, axis_at), (shards_of,), jnp.float32, low / len(cuts), largest / len(cuts)))
        level = level * jnp.repeat(heights, dims[axis_at] // shards_of).reshape([-1 if axis == axis_at else 1 for axis in range(len(dims))])
    return level


def profile(amount, total, bound, slope):
    loads = [(1 << 20) // math.isqrt(rank ** slope) + 1 for rank in range(2, amount + 1)]
    rest, holding = total - bound - (amount - 1), [1] * (amount - 1)
    while rest > 0:
        free = [i for i in range(amount - 1) if holding[i] < bound]
        whole, left = sum([loads[i] for i in free]), rest
        for i in free:
            extra = min(bound - holding[i], max(1, left * loads[i] // whole), rest)
            holding[i] = holding[i] + extra
            rest = rest - extra
    return np.array([bound] + holding)


def ragged_sizes(rng, number_of, total, reach, slope):
    if number_of == 2:
        one = jax.random.randint(rng, (), max(1, total - reach), min(reach, total - 1) + 1)
        return jnp.stack([one, total - one])
    tallies = jnp.asarray(profile(number_of, total, reach, slope), jnp.int32)
    twos = (number_of - 1) // 2
    giver, taker = tallies[1:1 + 2 * twos:2], tallies[2:2 + 2 * twos:2]
    slack = jnp.minimum(giver - 1, reach - taker)
    shifted = jax.random.randint(jax.random.fold_in(rng, 1), (twos,), 0, 1 << 20) % (slack + 1)
    tallies = tallies.at[1:1 + 2 * twos:2].set(giver - shifted).at[2:2 + 2 * twos:2].set(taker + shifted)
    return tallies[jax.random.permutation(jax.random.fold_in(rng, 2), number_of)]


def deal_out(stream_key, own, number, rows, number_of, top, limit, lean):
    order = jax.random.permutation(stream_key, number_of)
    heavy_load, common = shares(number_of, rows * top, limit, lean, True), shares(number_of, rows * top, limit, lean, False)
    places = jnp.arange(number_of)

    def named(sizes, turn):
        used = int((sizes > 0).sum())
        fixed = max(1, used // 4)
        shifted = fixed + (places - fixed + turn * (used - fixed)) % max(1, number_of - fixed)
        return jnp.zeros((number_of,), jnp.int32).at[order[jnp.where(places < fixed, places, shifted)]].set(jnp.asarray(sizes, jnp.int32))

    sizes = jnp.where(number % 4 == 0, named(heavy_load, number // 4), named(common, number - number // 4 - 1))
    mixed = jax.random.permutation(jax.random.fold_in(own, 3), number_of)
    source_of, taker = mixed[0:number_of // 2 * 2:2], mixed[1:number_of // 2 * 2:2]
    margin = jnp.minimum(sizes[source_of] - 1, limit - sizes[taker]) // 2
    margin = jnp.where((source_of == order[0]) | (taker == order[0]) | (sizes[taker] == 0), 0, jnp.maximum(margin, 0))
    shifted = jax.random.randint(jax.random.fold_in(own, 4), (number_of // 2,), 0, 1 << 20) % (margin + 1)
    sizes = sizes.at[source_of].add(-shifted).at[taker].add(shifted)
    members = jnp.searchsorted(jnp.cumsum(sizes), jnp.arange(rows * top), side="right").astype(jnp.int32)
    table = members.reshape(top, rows).T
    table = table[jax.random.permutation(jax.random.fold_in(own, 1), rows)]
    turn = jax.random.randint(jax.random.fold_in(own, 2), (rows, 1), 0, top)
    return jnp.take_along_axis(table, (jnp.arange(top)[None, :] + turn) % top, axis=1)


def shares(number_of, total, reach, slope, full):
    portions = [(1 << 20) // math.isqrt(grade ** slope) + 1 for grade in range(1, number_of + 1)]
    largest = reach if full else min(reach, max(-(-total // number_of), total * portions[0] // sum(portions)))
    least = 1 if total - largest >= number_of - 1 else 0
    holding, surplus = [largest] + [least] * (number_of - 1), total - largest - least * (number_of - 1)
    while surplus > 0:
        free = [i for i in range(1, number_of) if holding[i] < largest] or [i for i in range(1, number_of) if holding[i] < reach]
        pool, budget = sum([portions[i] for i in free]), surplus
        for i in free:
            addition = min(reach - holding[i], max(1, budget * portions[i] // pool), surplus)
            holding[i] = holding[i] + addition
            surplus = surplus - addition
    return np.array(holding)


def noise(key, extent, scale, bound, pieces=(), held_as=jnp.bfloat16):
    array = jax.random.normal(key, extent, jnp.float32) * scale
    if len(pieces) > 0:
        array = block_scale(key, extent, pieces, -0.22, 0.18) * array
    return jnp.clip(array, min=-bound, max=bound).astype(held_as)


def setup_inputs(seed: int = 0) -> dict:
    splits = jax.random.split(jax.random.key(seed), 19)
    tokens = noise(splits[0], (NSEQ, SEQ, D), 1.0, 6.0, ((0, 16), (1, 2)))
    segments = jax.vmap(lambda own: jnp.searchsorted(jnp.cumsum(ragged_sizes(own, 4, SEQ, SEQ // 2, 0)), jnp.arange(SEQ), side="right"))(jax.random.split(splits[1], NSEQ)).reshape((NSEQ, SEQ)).astype(jnp.int32)
    routes_keys = jax.random.split(jax.random.fold_in(splits[2], 1), NSEQ * SEQ // TDS)
    routes_turns = jax.random.permutation(jax.random.fold_in(splits[2], 3), NSEQ * SEQ // TDS)
    routes = jax.vmap(lambda own, number: deal_out(jax.random.fold_in(splits[2], 2), own, number, TDS, EXPERTS, TOP, CAPS, 2))(routes_keys, routes_turns).reshape((NSEQ, SEQ, TOP))
    combine = jnp.clip(0.05 + 0.35 * jax.random.uniform(splits[3], (NSEQ, SEQ, TOP), jnp.float32) ** block_scale(splits[3], (NSEQ, SEQ, TOP), ((0, 16), (1, 2)), -0.2, 0.2), 0.05, 0.4)
    input_gain = jnp.clip(1.0 + 0.18 * jax.random.normal(splits[4], (D,), jnp.float32), 0.099609375, 1.8984375).astype(jnp.bfloat16)
    query_weight = noise(splits[5], (D, HEADS * (NOPE + ROPE)), D ** -0.5, 0.125, ((0, 32),))
    latent_weight = noise(splits[6], (D, RANK + ROPE), D ** -0.5, 0.125, ((0, 32),))
    latent_gain = jnp.clip(1.0 + 0.18 * jax.random.normal(splits[7], (RANK,), jnp.float32), 0.099609375, 1.8984375).astype(jnp.bfloat16)
    expand_weight = noise(splits[8], (RANK, HEADS * (NOPE + VDIM)), RANK ** -0.5, 0.25, ((1, 32),))
    output_weight = noise(splits[9], (HEADS * VDIM, D), (HEADS * VDIM * 16 // SEQ) ** -0.5, 1.0, ((1, 32),))
    middle_gain = jnp.clip(1.0 + 0.18 * jax.random.normal(splits[10], (D,), jnp.float32), 0.099609375, 1.8984375).astype(jnp.bfloat16)
    shared_gate = noise(splits[11], (D, FS), D ** -0.5, 0.125, ((0, 32),))
    shared_up = noise(splits[12], (D, FS), D ** -0.5, 0.125, ((0, 32),))
    shared_down = noise(splits[13], (FS, D), FS ** -0.5, 0.109375, ((1, 32),))
    expert_gate = noise(splits[14], (EXPERTS, D, FE), D ** -0.5, 0.125, ((0, 16), (1, 2)))
    expert_up = noise(splits[15], (EXPERTS, D, FE), D ** -0.5, 0.125, ((0, 16), (1, 2)))
    expert_down = noise(splits[16], (EXPERTS, FE, D), FE ** -0.5, 0.15625, ((0, 16), (2, 2)))
    cotangent = noise(splits[17], (NSEQ, SEQ, D), 1.0, 6.0, ((0, 16), (1, 2)))
    return {"tokens": tokens, "segments": segments, "routes": routes, "combine": combine, "input_gain": input_gain, "query_weight": query_weight, "latent_weight": latent_weight, "latent_gain": latent_gain, "expand_weight": expand_weight, "output_weight": output_weight, "middle_gain": middle_gain, "shared_gate": shared_gate, "shared_up": shared_up, "shared_down": shared_down, "expert_gate": expert_gate, "expert_up": expert_up, "expert_down": expert_down, "cotangent": cotangent}


@jax.custom_vjp
def low(v):
    return lax.optimization_barrier(v.astype(jnp.bfloat16)).astype(jnp.float32)

@jax.custom_vjp
def low_back(v):
    return v

def low_keep(v):
    return (low(v), None)

def low_pass(kept, grad):
    return (grad,)

def back_keep(v):
    return (v, None)

def back_low(kept, grad):
    return (low(grad),)
low.defvjp(low_keep, low_pass)
low_back.defvjp(back_keep, back_low)

def matmul(left_side, right_side):
    return jnp.dot(left_side, right_side, precision=lax.Precision.HIGHEST)

def rms_norm(values, gain_vec):
    scale_vec = lax.rsqrt(lax.optimization_barrier(jnp.mean(values * values, axis=-1, keepdims=True)) + 1e-06)
    return values * scale_vec * gain_vec

def rotary(values, cosine, sine_part):
    half_width = values.shape[-1] // 2
    first_half = values[..., :half_width]
    second_half = values[..., half_width:]
    return jnp.concatenate([first_half * cosine - second_half * sine_part, second_half * cosine + first_half * sine_part], axis=-1)

def attend(normed, doc_ids, query_weight, latent_weight, latent_gain, expand_weight, output_weight):
    places = jnp.arange(SEQ).astype(jnp.float32)
    frequency = jnp.power(10000.0, -jnp.arange(ROPE // 2).astype(jnp.float32) * 2.0 / ROPE)
    angles = places[:, None] * frequency[None, :]
    cosine = jnp.cos(angles)
    sine_part = jnp.sin(angles)
    query_linear = low_back(matmul(normed, query_weight)).reshape(SEQ, HEADS, NOPE + ROPE)
    queries = low(jnp.concatenate([query_linear[..., :NOPE], rotary(query_linear[..., NOPE:], cosine[:, None, :], sine_part[:, None, :])], axis=-1))
    latent_linear = low_back(matmul(normed, latent_weight))
    latent = low(rms_norm(latent_linear[:, :RANK], latent_gain))
    key_rope = low(rotary(latent_linear[:, RANK:], cosine, sine_part))
    key_value = low(low_back(matmul(latent, expand_weight))).reshape(SEQ, HEADS, NOPE + VDIM)
    key_all = jnp.concatenate([key_value[..., :NOPE], jnp.broadcast_to(key_rope[:, None, :], (SEQ, HEADS, ROPE))], axis=-1)
    logits = low_back(jnp.einsum('ihd,jhd->hij', queries, key_all, precision=lax.Precision.HIGHEST))
    position = jnp.arange(SEQ)
    allowed = (doc_ids[:, None] == doc_ids[None, :]) & (position[:, None] >= position[None, :])
    masked = jnp.where(allowed[None], logits * (NOPE + ROPE) ** (-0.5), -1e+30)
    row_max = lax.optimization_barrier(jnp.max(masked, axis=-1, keepdims=True))
    exponent = jnp.exp(masked - row_max)
    softmax_out = exponent / lax.optimization_barrier(jnp.sum(exponent, axis=-1, keepdims=True))
    mixed = low(low_back(jnp.einsum('hij,jhd->ihd', low(softmax_out), key_value[..., NOPE:], precision=lax.Precision.HIGHEST)))
    return low_back(matmul(mixed.reshape(SEQ, HEADS * VDIM), output_weight))

def layer(tokens, input_gain, query_weight, latent_weight, latent_gain, expand_weight, output_weight, middle_gain, shared_gate, shared_up, shared_down, expert_gate, expert_up, expert_down, segments, routes, combine):
    normed = low(rms_norm(tokens, input_gain))

    def one_sequence(pair_in):
        return attend(pair_in[0], pair_in[1], query_weight, latent_weight, latent_gain, expand_weight, output_weight)
    attention = lax.map(jax.checkpoint(one_sequence), (normed, segments))
    middle = tokens + attention
    flat_rows = low(rms_norm(middle, middle_gain)).reshape(-1, D)
    gate_pre = low_back(matmul(flat_rows, shared_gate))
    up_pre = low_back(matmul(flat_rows, shared_up))
    shared = low_back(matmul(low(jax.nn.silu(gate_pre) * up_pre), shared_down))
    dense_weights = lax.optimization_barrier(jnp.sum(combine[..., None] * jax.nn.one_hot(routes, EXPERTS, dtype=jnp.float32), axis=-2)).reshape(-1, EXPERTS)

    def one_expert(running, inputs):
        one_gate, one_up, one_down, column = inputs
        input_rows = low_back(flat_rows)
        gate_val = low_back(matmul(input_rows, one_gate))
        up_val = low_back(matmul(input_rows, one_up))
        expert_out = low(low_back(matmul(low(jax.nn.silu(gate_val) * up_val), one_down)))
        return (running + column[:, None] * expert_out, None)
    routed, _ = lax.scan(jax.checkpoint(one_expert), jnp.zeros_like(flat_rows), (expert_gate, expert_up, expert_down, dense_weights.T))
    return (middle.reshape(-1, D) + shared + routed).reshape(tokens.shape)

def reference(tokens, segments, routes, combine, input_gain, query_weight, latent_weight, latent_gain, expand_weight, output_weight, middle_gain, shared_gate, shared_up, shared_down, expert_gate, expert_up, expert_down, cotangent):
    floated = tuple((item.astype(jnp.float32) for item in (tokens, input_gain, query_weight, latent_weight, latent_gain, expand_weight, output_weight, middle_gain, shared_gate, shared_up, shared_down, expert_gate, expert_up, expert_down)))
    weights_route = combine.astype(jnp.float32)

    def forward(*values):
        return layer(*values, segments, routes, weights_route)
    result, pullback = jax.vjp(forward, *floated)
    gradients = pullback(cotangent.astype(jnp.float32))
    return (result.astype(jnp.bfloat16), gradients[0], gradients[1], gradients[2], gradients[3], gradients[4], gradients[5], gradients[6], gradients[7], gradients[8], gradients[9], gradients[10], gradients[11], gradients[12], gradients[13])
```

```python
import functools

import jax
import jax.numpy as jnp
from jax import lax
from jax.experimental import pallas as pl
from jax.experimental.pallas import tpu as pltpu
from jax.sharding import PartitionSpec as P

NOPE = 128
ROPE = 64
VDIM = 128
RANK = 512
DOC = 512
epsilon = 1e-06
f32 = jnp.float32
bf16 = jnp.bfloat16
MIB = 1 << 20


def mm(spec, a, b):
    return jnp.einsum(spec, a, b, preferred_element_type=f32)


def dot(a, b, ca, cb):
    return lax.dot_general(a, b, (((ca,), (cb,)), ((), ())), preferred_element_type=f32)


def after(values, earlier):
    return lax.optimization_barrier((values, earlier))[0]


def rotate(values, cosine, sine):
    half = values.shape[-1] // 2
    a, b = values[..., :half], values[..., half:]
    return jnp.concatenate([a * cosine - b * sine, b * cosine + a * sine], axis=-1)


def rotate_back(values, cosine, sine):
    return rotate(values, cosine, -sine)


def norm_back(gradient, normed, scale_vec, gain_vec):
    scaled = gradient * gain_vec
    inner = jnp.mean(scaled * normed, axis=-1, keepdims=True)
    return scale_vec * (scaled - normed * inner), jnp.sum(gradient * normed, axis=0)


def silu_parts(gate_in):
    sig = jax.nn.sigmoid(gate_in)
    return gate_in * sig, sig * (1.0 + gate_in * (1.0 - sig))


def rotary_tables(positions):
    frequency = jnp.power(10000.0, -jnp.arange(ROPE // 2).astype(f32) * 2.0 / ROPE)
    angles = positions.astype(f32)[:, None] * frequency[None, :]
    return jnp.cos(angles), jnp.sin(angles)


def window_start(block, rows, length, seq, reach):
    first = lax.axis_index("dp") * length + block * rows - DOC
    return jnp.clip(first, 0, seq - reach)


def swap_halves(values):
    lane = lax.broadcasted_iota(jnp.int32, values.shape, 1)
    up = pltpu.roll(values, ROPE // 2, 1)
    down = pltpu.roll(values, 2 * ROPE - ROPE // 2, 1)
    return jnp.where(lane % ROPE < ROPE // 2, down, up)


def head_lanes(shape, head):
    lane = lax.broadcasted_iota(jnp.int32, shape, 1)
    return (lane // ROPE) == head


def probabilities(q, qr, k, kr, bias):
    scores = (dot(q, k, 1, 1) + dot(qr, kr, 1, 1)) * (NOPE + ROPE) ** (-0.5) + bias
    exponent = jnp.exp(scores - jnp.max(scores, axis=-1, keepdims=True))
    return exponent / jnp.sum(exponent, axis=-1, keepdims=True)


def attend_kernel(sizes, nope_ref, rope_ref, cos_ref, sin_ref, kv_ref, kr_ref, bias_ref, out_ref):
    blocks, rows, length, seq, reach = sizes
    for block in range(blocks):
        at = pl.ds(block * rows, rows)
        rope = rope_ref[at, :]
        rope = (rope * cos_ref[at, :] + swap_halves(rope) * sin_ref[at, :]).astype(bf16)
        start = pl.multiple_of(window_start(block, rows, length, seq, reach), 128)
        span = pl.ds(start, reach)
        kr = kr_ref[span, :]
        for head in range(2):
            qr = jnp.where(head_lanes(rope.shape, head), rope, jnp.zeros_like(rope))
            q = nope_ref[at, head * NOPE : (head + 1) * NOPE].astype(bf16)
            k = kv_ref[span, head * 256 : head * 256 + NOPE]
            v = kv_ref[span, head * 256 + NOPE : (head + 1) * 256]
            probs = probabilities(q, qr, k, kr, bias_ref[block])
            out_ref[at, head * VDIM : (head + 1) * VDIM] = dot(
                probs.astype(bf16), v, 1, 0
            ).astype(bf16)


def attend_back_kernel(
    sizes,
    nope_ref,
    rope_ref,
    cos_ref,
    sin_ref,
    kv_ref,
    kr_ref,
    bias_ref,
    grad_ref,
    dnope_ref,
    drope_ref,
    dkv_ref,
    dkr_ref,
    dk_acc,
    dv_acc,
):
    blocks, rows, length, seq, reach = sizes
    factor = (NOPE + ROPE) ** (-0.5)

    @pl.when(pl.program_id(0) == 0)
    def _():
        dkr_ref[...] = jnp.zeros_like(dkr_ref)

    dk_acc[...] = jnp.zeros_like(dk_acc)
    dv_acc[...] = jnp.zeros_like(dv_acc)
    for block in range(blocks):
        at = pl.ds(block * rows, rows)
        rope = rope_ref[at, :]
        rope = (rope * cos_ref[at, :] + swap_halves(rope) * sin_ref[at, :]).astype(bf16)
        start = pl.multiple_of(window_start(block, rows, length, seq, reach), 128)
        span = pl.ds(start, reach)
        kr = kr_ref[span, :]
        rope_grad = jnp.zeros((rows, 2 * ROPE), f32)
        for head in range(2):
            mine = head_lanes(rope.shape, head)
            qr = jnp.where(mine, rope, jnp.zeros_like(rope))
            q = nope_ref[at, head * NOPE : (head + 1) * NOPE].astype(bf16)
            k = kv_ref[span, head * 256 : head * 256 + NOPE]
            v = kv_ref[span, head * 256 + NOPE : (head + 1) * 256]
            grad = grad_ref[at, head * VDIM : (head + 1) * VDIM]
            probs = probabilities(q, qr, k, kr, bias_ref[block])
            dprobs = dot(grad, v, 1, 1)
            inner = jnp.sum(dprobs * probs, axis=-1, keepdims=True)
            dscores = (probs * (dprobs - inner) * factor).astype(bf16)
            dnope_ref[at, head * NOPE : (head + 1) * NOPE] = dot(dscores, k, 1, 0).astype(bf16)
            rope_grad += jnp.where(mine, dot(dscores, kr, 1, 0), 0.0)
            dk_acc[head, span, :] += dot(dscores, q, 0, 0)
            dv_acc[head, span, :] += dot(probs.astype(bf16), grad, 0, 0)
            dkr_ref[span, :] += dot(dscores, qr, 0, 0)
        rope_grad = rope_grad * cos_ref[at, :] - swap_halves(rope_grad) * sin_ref[at, :]
        drope_ref[at, :] = rope_grad.astype(bf16)
    for head in range(2):
        dkv_ref[:, head * 256 : head * 256 + NOPE] = dk_acc[head].astype(bf16)
        dkv_ref[:, head * 256 + NOPE : (head + 1) * 256] = dv_acc[head].astype(bf16)


def attention_sizes(length, seq):
    rows = min(256, length)
    return length // rows, rows, length, seq, min(seq, rows + DOC)


def attention_specs(length, seq, heads, sizes):
    first_rope = heads * NOPE // (2 * ROPE)
    whole = lambda shape: pl.BlockSpec(shape, lambda p: (0,) * len(shape))
    return [
        pl.BlockSpec((length, 2 * NOPE), lambda p: (0, p)),
        pl.BlockSpec((length, 2 * ROPE), lambda p: (0, first_rope + p)),
        whole((length, 2 * ROPE)),
        whole((length, 2 * ROPE)),
        pl.BlockSpec((seq, 2 * (NOPE + VDIM)), lambda p: (0, p)),
        whole((seq, 2 * ROPE)),
        whole((sizes[0], sizes[1], sizes[4])),
    ]


def attend(linear, tables, kv, kr, bias, heads):
    length, seq = linear.shape[0], kv.shape[0]
    sizes = attention_sizes(length, seq)
    return pl.pallas_call(
        functools.partial(attend_kernel, sizes),
        grid=(heads // 2,),
        in_specs=attention_specs(length, seq, heads, sizes),
        out_specs=pl.BlockSpec((length, 2 * VDIM), lambda p: (0, p)),
        out_shape=jax.ShapeDtypeStruct((length, heads * VDIM), bf16),
        compiler_params=pltpu.CompilerParams(vmem_limit_bytes=48 * MIB),
        name="attend",
    )(linear, linear, *tables, kv, kr, bias)


def attend_back(linear, tables, kv, kr, bias, grad, heads):
    length, seq = linear.shape[0], kv.shape[0]
    sizes = attention_sizes(length, seq)
    return pl.pallas_call(
        functools.partial(attend_back_kernel, sizes),
        grid=(heads // 2,),
        in_specs=attention_specs(length, seq, heads, sizes)
        + [pl.BlockSpec((length, 2 * VDIM), lambda p: (0, p))],
        out_specs=[
            pl.BlockSpec((length, 2 * NOPE), lambda p: (0, p)),
            pl.BlockSpec((length, 2 * ROPE), lambda p: (0, p)),
            pl.BlockSpec((seq, 2 * (NOPE + VDIM)), lambda p: (0, p)),
            pl.BlockSpec((seq, 2 * ROPE), lambda p: (0, 0)),
        ],
        out_shape=[
            jax.ShapeDtypeStruct((length, heads * NOPE), bf16),
            jax.ShapeDtypeStruct((length, heads * ROPE), bf16),
            jax.ShapeDtypeStruct((seq, heads * (NOPE + VDIM)), bf16),
            jax.ShapeDtypeStruct((seq, 2 * ROPE), f32),
        ],
        scratch_shapes=[pltpu.VMEM((2, seq, NOPE), f32), pltpu.VMEM((2, seq, VDIM), f32)],
        compiler_params=pltpu.CompilerParams(vmem_limit_bytes=48 * MIB),
        name="attend_back",
    )(linear, linear, *tables, kv, kr, bias, grad)


def one_hot(place_ref, slots):
    place = place_ref[0]
    slot = lax.broadcasted_iota(jnp.int32, (slots, place.shape[1]), 0)
    return slot == place


def width_parts(refs, width):
    step = width // len(refs)
    return [(ref, pl.ds(i * step, step)) for i, ref in enumerate(refs)]


def forward_kernel(n, slots, place_ref, rows_ref, *refs):
    weights, shared, outs = refs[:n], refs[n : 2 * n], refs[2 * n :]
    picked_ref, act_ref, up_slope_ref, silu_ref, act_s_ref, up_slope_s_ref, silu_s_ref = outs
    width = rows_ref.shape[-1]
    picks = one_hot(place_ref, slots).astype(f32).astype(bf16)
    picked_ref[0] = dot(picks, rows_ref[0], 1, 0).astype(bf16)
    both = total([dot(picked_ref[0, :, at], w[...], 1, 0) for w, at in width_parts(weights, width)])
    half = both.shape[1] // 2
    silu, slope = silu_parts(both[:, :half])
    up = both[:, half:]
    act_ref[0] = (silu * up).astype(bf16)
    up_slope_ref[0] = (up * slope).astype(bf16)
    silu_ref[0] = silu.astype(bf16)
    both = total([dot(rows_ref[0, :, at], w[...], 1, 0) for w, at in width_parts(shared, width)])
    half = both.shape[1] // 2
    silu, slope = silu_parts(both[:, :half])
    up = both[:, half:]
    act_s_ref[0] = (silu * up).astype(bf16)
    up_slope_s_ref[0] = (up * slope).astype(bf16)
    silu_s_ref[0] = silu.astype(bf16)


def backward_kernel(
    n, slots, place_ref, weight_ref, grads_ref, us_ref, silu_ref, us_s_ref, silu_s_ref, *refs
):
    gate_up, down, gate_up_s, down_s = (refs[i * n : (i + 1) * n] for i in range(4))
    picked_ref, d_gate_ref, d_up_ref, d_shared_ref, d_rows_ref = refs[4 * n :]
    width = grads_ref.shape[-1]
    hot = one_hot(place_ref, slots)
    slot_weight = jnp.sum(jnp.where(hot, weight_ref[0], 0.0), axis=1, keepdims=True)
    picks = hot.astype(f32).astype(bf16)
    picked_ref[0] = (dot(picks, grads_ref[0], 1, 0) * slot_weight).astype(bf16)
    d_act = total([dot(picked_ref[0, :, at], w[...], 1, 1) for w, at in width_parts(down, width)])
    d_gate = (d_act * us_ref[0].astype(f32)).astype(bf16)
    d_up = (d_act * silu_ref[0].astype(f32)).astype(bf16)
    d_gate_ref[0] = d_gate
    d_up_ref[0] = d_up
    d_both = jnp.concatenate([d_gate, d_up], axis=1)
    d_act = total([dot(grads_ref[0, :, at], w[...], 1, 0) for w, at in width_parts(down_s, width)])
    half = d_act.shape[1]
    d_shared_ref[0, :, :half] = (d_act * us_s_ref[0].astype(f32)).astype(bf16)
    d_shared_ref[0, :, half:] = (d_act * silu_s_ref[0].astype(f32)).astype(bf16)
    for (w, at), w_s in zip(width_parts(gate_up, width), gate_up_s):
        d_row = dot(d_both, w[...], 1, 1).astype(bf16)
        d_rows_ref[0, :, at] = (
            dot(picks, d_row, 0, 0) + dot(d_shared_ref[0], w_s[...], 1, 1)
        ).astype(bf16)


def output_kernel(n, slots, place_ref, weight_ref, act_ref, act_s_ref, *refs):
    down, down_s, out_ref = refs[:n], refs[n : 2 * n], refs[2 * n]
    width = out_ref.shape[-1]
    hot = one_hot(place_ref, slots)
    slot_weight = jnp.sum(jnp.where(hot, weight_ref[0], 0.0), axis=1, keepdims=True)
    picks = hot.astype(f32).astype(bf16)
    for (w, at), w_s in zip(width_parts(down, width), down_s):
        out = (dot(act_ref[0], w[...], 1, 0) * slot_weight).astype(bf16)
        out_ref[0, :, at] = (
            dot(picks, out, 0, 0) + dot(act_s_ref[0], w_s[...], 1, 1)
        ).astype(bf16)


def by_block(kernel, name, blocked, fixed, outs, flops):
    count = blocked[0].shape[0]
    block = lambda a: pl.BlockSpec((1, *a.shape[1:]), lambda b: (b, 0, 0))
    stay = lambda a: pl.BlockSpec(a.shape, lambda b: (0, 0), pipeline_mode=pl.Buffered(1))
    moved = sum(a.size * a.dtype.itemsize for a in (*blocked, *fixed, *outs))
    return pl.pallas_call(
        kernel,
        grid=(count,),
        in_specs=[block(a) for a in blocked] + [stay(a) for a in fixed],
        out_specs=[block(a) for a in outs],
        out_shape=outs,
        compiler_params=pltpu.CompilerParams(vmem_limit_bytes=60 * MIB),
        cost_estimate=pl.CostEstimate(flops=flops, bytes_accessed=moved, transcendentals=0),
        name=name,
    )(*blocked, *fixed)


def add_rows(into, left, right):
    step = 16
    lead = (slice(None),) * (len(into.shape) - 2)

    @pl.loop(0, into.shape[-2] // step)
    def _(i):
        at = (*lead, pl.ds(pl.multiple_of(i * step, step), step), slice(None))
        into[at] = (left[at].astype(f32) + right[at].astype(f32)).astype(into.dtype)


def grad_sum_kernel(chunks, n, *refs):
    ins, outs = refs[:n], refs[n : 2 * n]
    own, got, load_sem, send_sem, recv_sem = refs[2 * n], refs[2 * n + 1 : 2 * n + 6], *refs[2 * n + 6 :]
    dp, expert = lax.axis_index("dp"), lax.axis_index("expert")
    core, y = expert % 2, (expert // 2) % 2
    z_low, z_high = (expert // 4) % 2, expert // 8
    partners = [
        {"expert": expert + 1 - 2 * core},
        {"dp": 1 - dp},
        {"expert": expert + 2 - 4 * y},
        {"expert": expert + 4 - 8 * z_low},
        {"expert": expert + 8 - 16 * z_high},
    ]
    barrier = pltpu.get_barrier_semaphore()
    for partner in partners:
        pl.semaphore_signal(barrier, inc=1, device_id=partner, device_id_type=pl.DeviceIdType.MESH)
    pl.semaphore_wait(barrier, len(partners))
    count = len(chunks)

    def source(k, which):
        array, start, wide = chunks[k]
        return ins[array].at[:, :, :, :, which, :, pl.ds(start, wide)]

    def cut(ref, k):
        return ref.at[(slice(None),) * (len(ref.shape) - 1) + (pl.ds(0, chunks[k][2]),)]

    def send(stage, k, values):
        return pltpu.make_async_remote_copy(
            src_ref=values,
            dst_ref=cut(got[stage].at[k], k),
            send_sem=send_sem.at[stage, k],
            recv_sem=recv_sem.at[stage, k],
            device_id=partners[stage],
            device_id_type=pl.DeviceIdType.MESH,
        )

    def load(k):
        return pltpu.make_async_copy(source(k, core), cut(own.at[k % 2], k), load_sem.at[k % 2])

    copies = {}

    def start(stage, k, values):
        copies[stage, k] = send(stage, k, values)
        copies[stage, k].start()

    for k in range(count):
        start(0, k, source(k, 1 - core))
    for k in range(min(2, count)):
        load(k).start()
    for turn in range(count + 4):
        k = turn
        if k < count:
            load(k).wait()
            copies[0, k].wait_recv()
            held, mine = cut(got[0].at[k], k), cut(own.at[k % 2], k)
            add_rows(held.at[1 - dp], held.at[1 - dp], mine.at[1 - dp])
            start(1, k, held.at[1 - dp])
            add_rows(held.at[dp], held.at[dp], mine.at[dp])
            if k + 2 < count:
                load(k + 2).start()
        k = turn - 1
        if 0 <= k < count:
            copies[1, k].wait_recv()
            held = cut(got[1].at[k], k)
            add_rows(held, held, cut(got[0].at[k], k).at[dp])
            start(2, k, held.at[:, :, 1 - y])
        k = turn - 2
        if 0 <= k < count:
            copies[2, k].wait_recv()
            held = cut(got[2].at[k], k)
            add_rows(held, held, cut(got[1].at[k], k).at[:, :, y])
            start(3, k, held.at[:, 1 - z_low])
        k = turn - 3
        if 0 <= k < count:
            copies[3, k].wait_recv()
            held = cut(got[3].at[k], k)
            add_rows(held, held, cut(got[2].at[k], k).at[:, z_low])
            start(4, k, held.at[1 - z_high])
        k = turn - 4
        if 0 <= k < count:
            copies[4, k].wait_recv()
            array, first, wide = chunks[k]
            add_rows(
                outs[array].at[:, pl.ds(first, wide)],
                cut(got[4].at[k], k),
                cut(got[3].at[k], k).at[z_high],
            )
    for copy in copies.values():
        copy.wait_send()


def grad_sums(arrays):
    shards = 32
    rows, piece = arrays[0].shape[0] // shards, 1024
    chunks = [
        (i, at, min(piece, a.shape[1] - at))
        for i, a in enumerate(arrays)
        for at in range(0, a.shape[1], piece)
    ]
    dims = (2, 2, 2, 2)
    count = len(chunks)
    return pl.pallas_call(
        functools.partial(grad_sum_kernel, chunks, len(arrays)),
        in_specs=[pl.BlockSpec(memory_space=pl.ANY)] * len(arrays),
        out_specs=[pl.BlockSpec(memory_space=pltpu.VMEM)] * len(arrays),
        out_shape=[jax.ShapeDtypeStruct((rows, a.shape[1]), f32) for a in arrays],
        scratch_shapes=[
            pltpu.VMEM((2, *dims, rows, piece), bf16),
            *[pltpu.VMEM((count, *dims[i:], rows, piece), bf16) for i in range(5)],
            pltpu.SemaphoreType.DMA((2,)),
            pltpu.SemaphoreType.DMA((5, count)),
            pltpu.SemaphoreType.DMA((5, count)),
        ],
        compiler_params=pltpu.CompilerParams(
            collective_id=1, has_side_effects=True, vmem_limit_bytes=52 * MIB
        ),
        name="grad_sums",
    )(*[a.reshape(*dims, 2, rows, a.shape[1]) for a in arrays])


def swap(values):
    return lax.ppermute(values, "dp", [(0, 1), (1, 0)])


def turned(values, dp_count):
    if dp_count != 2:
        return values
    half = values.shape[-1] // 2
    a, b = values[..., :half], values[..., half:]
    first = lax.axis_index("dp") == 0
    return jnp.concatenate([jnp.where(first, a, b), jnp.where(first, b, a)], axis=-1)


def weight_parts(values, axis, dp_count):
    if dp_count != 2:
        return [lax.all_gather(values, "dp", axis=axis, tiled=True)]
    return [values, swap(values)]


def scatter_dp(results, axis):
    if len(results) == 1:
        return lax.psum_scatter(
            results[0]().astype(bf16), "dp", scatter_dimension=axis, tiled=True
        ).astype(f32)
    sent = swap(results[1]().astype(bf16))
    return results[0]() + sent.astype(f32)


def total(terms):
    return functools.reduce(jnp.add, terms)


def heads_apart(values, heads):
    by_head = values.reshape(-1, heads, NOPE + ROPE)
    rows = values.shape[0]
    return jnp.concatenate(
        [by_head[..., :NOPE].reshape(rows, -1), by_head[..., NOPE:].reshape(rows, -1)], axis=1
    )


def heads_together(values, heads):
    rows = values.shape[0]
    nope = values[:, : heads * NOPE].reshape(rows, heads, NOPE)
    rope = values[:, heads * NOPE :].reshape(rows, heads, ROPE)
    return jnp.concatenate([nope, rope], axis=-1).reshape(rows, -1)


def local(
    tokens,
    segments,
    routes,
    combine,
    input_gain,
    query_weight,
    latent_weight,
    latent_gain,
    expand_weight,
    output_weight,
    middle_gain,
    shared_gate,
    shared_up,
    shared_down,
    expert_gate,
    expert_up,
    expert_down,
    cotangent,
):
    _, length, width = tokens.shape
    seq = segments.shape[1]
    top_k = routes.shape[2]
    dp_count = lax.axis_size("dp")
    groups = lax.axis_size("expert")
    shards = dp_count * groups
    both = ("dp", "expert")
    hidden_s = shared_gate.shape[1]
    part_s = hidden_s // groups
    slots = length * top_k * 4 // (groups * 3)
    offset = lax.axis_index("dp") * length
    query_width = query_weight.shape[1]
    heads = query_width // (NOPE + ROPE)
    rows_w = query_weight.shape[0]

    g1 = input_gain.shape[0]
    gains = jnp.concatenate([input_gain, middle_gain, latent_gain])
    gains = lax.all_gather(gains, both, axis=0, tiled=False)
    first_gain = gains[:, :g1].reshape(-1).astype(f32)
    second_gain = gains[:, g1 : 2 * g1].reshape(-1).astype(f32)
    latent_norm = gains[:, 2 * g1 :].reshape(-1).astype(f32)

    hits = routes[0][:, None, :] == jnp.arange(groups, dtype=jnp.int32)[None, :, None]
    dense = jnp.sum(jnp.where(hits, combine[0][:, None, :], 0.0), axis=-1)
    dense = jnp.where(jnp.any(hits, axis=-1), dense, -1.0)
    my_weights = lax.all_to_all(dense.T, "expert", split_axis=0, concat_axis=0, tiled=True)
    chosen = my_weights >= 0.0
    before = jnp.arange(length)[:, None] < jnp.arange(length)[None, :]
    place = mm("bt,ts->bs", chosen.astype(bf16), before.astype(bf16)).astype(jnp.int32)
    place = jnp.where(chosen, place, -1)
    place = place[:, None, :]
    row_weights = my_weights[:, None, :]

    expand_rows = expand_weight.T.shape[0]
    split = expand_rows // rows_w
    expand_wide = jnp.concatenate(jnp.split(expand_weight.T, split, axis=0), axis=1)
    gathered = lax.all_gather(
        jnp.concatenate([heads_apart(query_weight, heads), latent_weight, expand_wide], axis=1),
        both,
        axis=0,
        tiled=True,
    )
    linear_width = query_width + RANK + ROPE
    query_latent = gathered[:, :linear_width]
    expand_t = (
        gathered[:, linear_width:]
        .reshape(shards, rows_w, split, RANK)
        .transpose(0, 2, 1, 3)
        .reshape(-1, RANK)
    )
    output_t = lax.all_gather(output_weight.T, both, axis=0, tiled=True)

    shared_own = jnp.stack(
        [
            shared_gate.reshape(rows_w, groups, part_s),
            shared_up.reshape(rows_w, groups, part_s),
            shared_down.T.reshape(rows_w, groups, part_s),
        ],
        axis=1,
    ).transpose(2, 0, 1, 3)
    shared_cols = lax.all_to_all(shared_own, "expert", split_axis=0, concat_axis=0, tiled=True)
    shared_cols = weight_parts(shared_cols.reshape(groups * rows_w, 3 * part_s), 0, dp_count)
    padded_s = -(-part_s // 128) * 128
    wide_s = [
        jnp.pad(c.reshape(-1, 3, part_s), ((0, 0), (0, 0), (0, padded_s - part_s)))
        for c in shared_cols
    ]
    gate_up_s = [c[:, :2].reshape(-1, 2 * padded_s) for c in wide_s]
    down_s_t = [c[:, 2] for c in wide_s]

    first_gain, my_weights, gate_up_s, down_s_t, query_latent = lax.optimization_barrier(
        (first_gain, my_weights, gate_up_s, down_s_t, query_latent)
    )
    own_e = after((expert_gate[0], expert_up[0], expert_down[0]), query_latent)
    gate_up_e = weight_parts(jnp.concatenate(own_e[:2], axis=1), 0, dp_count)
    down_e = weight_parts(own_e[2], 1, dp_count)

    token_values = tokens[0].astype(f32)
    scale_one = lax.rsqrt(jnp.mean(token_values * token_values, axis=-1, keepdims=True) + epsilon)
    normed_one = token_values * scale_one
    normed_low = (normed_one * first_gain).astype(bf16)
    own_pos = offset + jnp.arange(length, dtype=jnp.int32)
    cosine, sine = rotary_tables(own_pos)
    tables = (
        jnp.concatenate([cosine] * 4, axis=1),
        jnp.concatenate([-sine, sine, -sine, sine], axis=1),
    )
    linear = mm("rd,dk->rk", normed_low, query_latent)
    latent_raw = linear[:, query_width : query_width + RANK]
    latent_scale = lax.rsqrt(jnp.mean(latent_raw * latent_raw, axis=-1, keepdims=True) + epsilon)
    latent_normed = latent_raw * latent_scale
    latent_low = (latent_normed * latent_norm).astype(bf16)
    rope_low = rotate(linear[:, query_width + RANK :], cosine, sine).astype(bf16)
    latent_rope = jnp.concatenate([latent_low, rope_low], axis=-1)
    if dp_count == 2:
        other = swap(latent_rope)
        is_first = lax.axis_index("dp") == 0
        latent_rope = jnp.concatenate(
            [jnp.where(is_first, latent_rope, other), jnp.where(is_first, other, latent_rope)]
        )
    else:
        latent_rope = lax.all_gather(latent_rope, "dp", axis=0, tiled=True)
    latent_all = latent_rope[:, :RANK]
    rope_keys = jnp.concatenate([latent_rope[:, RANK:]] * 2, axis=1)
    expanded = mm("rc,kc->rk", latent_all, expand_t).astype(bf16)
    blocks, block_rows, _, _, reach = attention_sizes(length, seq)
    bias = []
    for block in range(blocks):
        start = window_start(block, block_rows, length, seq, reach)
        q_pos = offset + block * block_rows + jnp.arange(block_rows)
        q_seg = lax.dynamic_slice_in_dim(segments[0], offset + block * block_rows, block_rows)
        k_seg = lax.dynamic_slice_in_dim(segments[0], start, reach)
        seen = (q_seg[:, None] == k_seg[None, :]) & (
            q_pos[:, None] >= (start + jnp.arange(reach))[None, :]
        )
        bias.append(jnp.where(seen, 0.0, -1e30).astype(f32))
    bias = jnp.stack(bias)
    mixed = attend(linear, tables, expanded, rope_keys, bias, heads)
    middle = token_values + mm("rv,dv->rd", mixed, output_t)
    scale_two = lax.rsqrt(jnp.mean(middle * middle, axis=-1, keepdims=True) + epsilon)
    normed_two = middle * scale_two
    ffn_rows = (normed_two * second_gain).astype(bf16)

    def gather_rows(values):
        return lax.all_gather(values, "expert", axis=0, tiled=False)

    grads_all = gather_rows(turned(cotangent[0], dp_count))
    rows_all = gather_rows(turned(ffn_rows, dp_count))

    n = len(gate_up_e)
    hidden = expert_gate.shape[2]
    block_of = lambda rows, columns: jax.ShapeDtypeStruct((groups, rows, columns), bf16)
    wide = [block_of(slots, hidden)] * 3
    wide_shared = [block_of(length, padded_s)] * 3
    unit = 2 * groups * width
    picked, act_e, up_slope, silu, act_s, up_slope_s, silu_s = by_block(
        functools.partial(forward_kernel, n, slots),
        "experts_forward",
        [place, rows_all],
        [*gate_up_e, *gate_up_s],
        [block_of(slots, width), *wide, *wide_shared],
        unit * (slots * (length + 2 * hidden) + 2 * length * padded_s),
    )
    picked_grad, d_gate, d_up, d_shared, d_rows_part = by_block(
        functools.partial(backward_kernel, n, slots),
        "experts_backward",
        [place, row_weights, grads_all, up_slope, silu, up_slope_s, silu_s],
        [*gate_up_e, *down_e, *gate_up_s, *down_s_t],
        [
            block_of(slots, width),
            *wide[:2],
            block_of(length, 2 * padded_s),
            block_of(length, width),
        ],
        unit * (slots * (2 * length + 3 * hidden) + 3 * length * padded_s),
    )
    [out_part] = by_block(
        functools.partial(output_kernel, n, slots),
        "experts_output",
        [place, row_weights, act_e, act_s],
        [*down_e, *down_s_t],
        [block_of(length, width)],
        unit * (slots * (length + hidden) + length * padded_s),
    )

    def flat(values):
        return values.reshape(-1, values.shape[-1])

    def scatter_rows(values):
        return lax.psum_scatter(flat(values), "expert", scatter_dimension=0, tiled=True)

    d_rows = scatter_rows(d_rows_part)

    column_parts = lambda values: jnp.split(flat(values), n, axis=1)
    picked, picked_grad, rows_parts, grads_parts = map(
        column_parts, (picked, picked_grad, rows_all, grads_all)
    )
    act_e, act_s, d_gate, d_up, d_shared = map(flat, (act_e, act_s, d_gate, d_up, d_shared))
    grad_gate_e = scatter_dp([lambda p=p: mm("rd,rf->df", p, d_gate) for p in picked], 0)
    grad_up_e = scatter_dp([lambda p=p: mm("rd,rf->df", p, d_up) for p in picked], 0)
    grad_down_e = scatter_dp([lambda p=p: mm("rf,rd->fd", act_e, p) for p in picked_grad], 1)
    grad_s = scatter_dp(
        [
            lambda r=r, g=g: jnp.concatenate(
                [mm("rd,rf->df", r, d_shared), mm("rd,rf->df", g, act_s)], axis=1
            )
            for r, g in zip(rows_parts, grads_parts)
        ],
        0,
    )
    grad_s = grad_s.reshape(groups, rows_w, 3, padded_s)[..., :part_s].astype(bf16)
    grad_s = lax.all_to_all(grad_s, "expert", split_axis=0, concat_axis=0, tiled=True)
    grad_s = grad_s.transpose(2, 1, 0, 3).reshape(3, rows_w, hidden_s).astype(f32)
    d_rows, grad_gate_e, grad_up_e, grad_down_e, grad_s, out_part = lax.optimization_barrier(
        (d_rows, grad_gate_e, grad_up_e, grad_down_e, grad_s, out_part)
    )
    d_rows_own = turned(d_rows, dp_count).astype(f32)

    out_grad = cotangent[0].astype(f32)
    middle_part, second_gain_grad = norm_back(d_rows_own, normed_two, scale_two, second_gain)
    middle_grad = out_grad + middle_part
    attn_grad = middle_grad.astype(bf16)
    mixed_grad = mm("rd,dv->rv", attn_grad, output_t).astype(bf16)
    grad_out_t = mm("rd,rv->dv", attn_grad, mixed).astype(bf16)
    out_sum = scatter_rows(after(out_part, d_rows))
    d_nope, d_rope, d_expanded, d_keys_rope = attend_back(
        linear, tables, expanded, rope_keys, bias, mixed_grad, heads
    )
    latent_part = mm("rk,kc->rc", d_expanded, expand_t)
    rope_part = d_keys_rope[:, :ROPE] + d_keys_rope[:, ROPE:]
    latent_rope_part = jnp.concatenate([latent_part, rope_part], axis=-1)
    if dp_count == 2:
        first_half, second_half = latent_rope_part[:length], latent_rope_part[length:]
        is_first = lax.axis_index("dp") == 0
        sent = swap(jnp.where(is_first, second_half, first_half).astype(bf16))
        combined = jnp.where(is_first, first_half, second_half) + sent.astype(f32)
    else:
        combined = lax.psum_scatter(latent_rope_part, "dp", scatter_dimension=0, tiled=True)
    grad_expand_t = mm("rk,rc->kc", d_expanded, latent_all).astype(bf16)
    latent_grad, latent_gain_grad = norm_back(
        combined[:, :RANK], latent_normed, latent_scale, latent_norm
    )
    rope_grad = rotate_back(combined[:, RANK:], cosine, sine)
    linear_grad = jnp.concatenate(
        [d_nope, d_rope, latent_grad.astype(bf16), rope_grad.astype(bf16)], axis=-1
    )
    normed_grad = mm("rk,dk->rd", linear_grad, query_latent)
    linear_grad = jnp.pad(linear_grad, ((0, 0), (0, -linear_width % 128)))
    input_part, first_gain_grad = norm_back(normed_grad, normed_one, scale_one, first_gain)
    tokens_grad = (middle_grad + input_part)[None]
    small = jnp.stack(
        [
            first_gain_grad,
            second_gain_grad,
            jnp.pad(
                latent_gain_grad.reshape(shards, -1), ((0, 0), (0, g1 - RANK // shards))
            ).reshape(-1),
        ],
        axis=1,
    )
    small = jnp.pad(small, ((0, 0), (0, -small.shape[1] % 128))).astype(bf16)
    grad_linear = mm("rd,rk->dk", normed_low, linear_grad).astype(bf16)
    grad_expand = (
        grad_expand_t.reshape(shards, split, rows_w, RANK)
        .transpose(0, 2, 1, 3)
        .reshape(width, split * RANK)
    )
    sums = [grad_out_t, grad_expand, grad_linear, small]
    if dp_count == 2 and groups == 16:
        sums = grad_sums(sums)
    else:
        sums = [
            lax.psum_scatter(v, both, scatter_dimension=0, tiled=True).astype(f32) for v in sums
        ]
    grad_out_t, grad_expand, grad_linear, small = sums
    grad_expand_t = jnp.concatenate(jnp.split(grad_expand, split, axis=1), axis=0)
    out_sum = after(out_sum, grad_linear)
    outputs = (middle + turned(out_sum, dp_count).astype(f32)).astype(bf16)[None]
    return (
        outputs,
        tokens_grad,
        small[:, 0],
        heads_together(grad_linear[:, :query_width], heads),
        grad_linear[:, query_width:linear_width],
        small[: RANK // shards, 2],
        grad_expand_t.T,
        grad_out_t.T,
        small[:, 1],
        grad_s[0],
        grad_s[1],
        grad_s[2].T,
        grad_gate_e[None],
        grad_up_e[None],
        grad_down_e[None],
    )


def solution(mesh):
    rows = P("expert", "dp", None)
    first = P(("dp", "expert"), None)
    last = P(None, ("dp", "expert"))
    vector = P(("dp", "expert"))
    down = P("expert", None, "dp")
    return jax.shard_map(
        local,
        mesh=mesh,
        in_specs=(
            rows,
            P("expert", None),
            rows,
            rows,
            vector,
            first,
            first,
            vector,
            last,
            last,
            vector,
            first,
            first,
            last,
            rows,
            rows,
            down,
            rows,
        ),
        out_specs=(
            rows,
            rows,
            vector,
            first,
            first,
            vector,
            last,
            last,
            vector,
            first,
            first,
            last,
            rows,
            rows,
            down,
        ),
        check_vma=False,
    )
```

```python
import functools

import jax
import jax.numpy as jnp
from jax import lax
from jax.experimental import pallas as pl
from jax.experimental.pallas import tpu as pltpu
from jax.sharding import PartitionSpec as P

NOPE = 128
ROPE = 64
VDIM = 128
RANK = 512
DOC = 512
epsilon = 1e-06
f32 = jnp.float32
bf16 = jnp.bfloat16
MIB = 1 << 20


def mm(spec, a, b):
    return jnp.einsum(spec, a, b, preferred_element_type=f32)


def dot(a, b, ca, cb):
    return lax.dot_general(a, b, (((ca,), (cb,)), ((), ())), preferred_element_type=f32)


def after(values, earlier):
    return lax.optimization_barrier((values, earlier))[0]


def rotate(values, cosine, sine):
    half = values.shape[-1] // 2
    a, b = values[..., :half], values[..., half:]
    return jnp.concatenate([a * cosine - b * sine, b * cosine + a * sine], axis=-1)


def rotate_back(values, cosine, sine):
    return rotate(values, cosine, -sine)


def norm_back(gradient, normed, scale_vec, gain_vec):
    scaled = gradient * gain_vec
    inner = jnp.mean(scaled * normed, axis=-1, keepdims=True)
    return scale_vec * (scaled - normed * inner), jnp.sum(gradient * normed, axis=0)


def silu_parts(gate_in):
    sig = jax.nn.sigmoid(gate_in)
    return gate_in * sig, sig * (1.0 + gate_in * (1.0 - sig))


def rotary_tables(positions):
    frequency = jnp.power(10000.0, -jnp.arange(ROPE // 2).astype(f32) * 2.0 / ROPE)
    angles = positions.astype(f32)[:, None] * frequency[None, :]
    return jnp.cos(angles), jnp.sin(angles)


def window_start(block, rows, length, seq, reach):
    first = lax.axis_index("dp") * length + block * rows - DOC
    return jnp.clip(first, 0, seq - reach)


def swap_halves(values):
    lane = lax.broadcasted_iota(jnp.int32, values.shape, 1)
    up = pltpu.roll(values, ROPE // 2, 1)
    down = pltpu.roll(values, 2 * ROPE - ROPE // 2, 1)
    return jnp.where(lane % ROPE < ROPE // 2, down, up)


def head_lanes(shape, head):
    lane = lax.broadcasted_iota(jnp.int32, shape, 1)
    return (lane // ROPE) == head


def probabilities(q, qr, k, kr, bias):
    scores = (dot(q, k, 1, 1) + dot(qr, kr, 1, 1)) * (NOPE + ROPE) ** (-0.5) + bias
    exponent = jnp.exp(scores - jnp.max(scores, axis=-1, keepdims=True))
    return exponent / jnp.sum(exponent, axis=-1, keepdims=True)


def attend_kernel(sizes, nope_ref, rope_ref, cos_ref, sin_ref, kv_ref, kr_ref, bias_ref, out_ref):
    blocks, rows, length, seq, reach = sizes
    for block in range(blocks):
        at = pl.ds(block * rows, rows)
        rope = rope_ref[at, :]
        rope = (rope * cos_ref[at, :] + swap_halves(rope) * sin_ref[at, :]).astype(bf16)
        start = pl.multiple_of(window_start(block, rows, length, seq, reach), 128)
        span = pl.ds(start, reach)
        kr = kr_ref[span, :]
        for head in range(2):
            qr = jnp.where(head_lanes(rope.shape, head), rope, jnp.zeros_like(rope))
            q = nope_ref[at, head * NOPE : (head + 1) * NOPE].astype(bf16)
            k = kv_ref[span, head * 256 : head * 256 + NOPE]
            v = kv_ref[span, head * 256 + NOPE : (head + 1) * 256]
            probs = probabilities(q, qr, k, kr, bias_ref[block])
            out_ref[at, head * VDIM : (head + 1) * VDIM] = dot(
                probs.astype(bf16), v, 1, 0
            ).astype(bf16)


def attend_back_kernel(
    sizes,
    nope_ref,
    rope_ref,
    cos_ref,
    sin_ref,
    kv_ref,
    kr_ref,
    bias_ref,
    grad_ref,
    dnope_ref,
    drope_ref,
    dkv_ref,
    dkr_ref,
    dk_acc,
    dv_acc,
):
    blocks, rows, length, seq, reach = sizes
    factor = (NOPE + ROPE) ** (-0.5)

    @pl.when(pl.program_id(0) == 0)
    def _():
        dkr_ref[...] = jnp.zeros_like(dkr_ref)

    dk_acc[...] = jnp.zeros_like(dk_acc)
    dv_acc[...] = jnp.zeros_like(dv_acc)
    for block in range(blocks):
        at = pl.ds(block * rows, rows)
        rope = rope_ref[at, :]
        rope = (rope * cos_ref[at, :] + swap_halves(rope) * sin_ref[at, :]).astype(bf16)
        start = pl.multiple_of(window_start(block, rows, length, seq, reach), 128)
        span = pl.ds(start, reach)
        kr = kr_ref[span, :]
        rope_grad = jnp.zeros((rows, 2 * ROPE), f32)
        for head in range(2):
            mine = head_lanes(rope.shape, head)
            qr = jnp.where(mine, rope, jnp.zeros_like(rope))
            q = nope_ref[at, head * NOPE : (head + 1) * NOPE].astype(bf16)
            k = kv_ref[span, head * 256 : head * 256 + NOPE]
            v = kv_ref[span, head * 256 + NOPE : (head + 1) * 256]
            grad = grad_ref[at, head * VDIM : (head + 1) * VDIM]
            probs = probabilities(q, qr, k, kr, bias_ref[block])
            dprobs = dot(grad, v, 1, 1)
            inner = jnp.sum(dprobs * probs, axis=-1, keepdims=True)
            dscores = (probs * (dprobs - inner) * factor).astype(bf16)
            dnope_ref[at, head * NOPE : (head + 1) * NOPE] = dot(dscores, k, 1, 0).astype(bf16)
            rope_grad += jnp.where(mine, dot(dscores, kr, 1, 0), 0.0)
            dk_acc[head, span, :] += dot(dscores, q, 0, 0)
            dv_acc[head, span, :] += dot(probs.astype(bf16), grad, 0, 0)
            dkr_ref[span, :] += dot(dscores, qr, 0, 0)
        rope_grad = rope_grad * cos_ref[at, :] - swap_halves(rope_grad) * sin_ref[at, :]
        drope_ref[at, :] = rope_grad.astype(bf16)
    for head in range(2):
        dkv_ref[:, head * 256 : head * 256 + NOPE] = dk_acc[head].astype(bf16)
        dkv_ref[:, head * 256 + NOPE : (head + 1) * 256] = dv_acc[head].astype(bf16)


def attention_sizes(length, seq):
    rows = min(256, length)
    return length // rows, rows, length, seq, min(seq, rows + DOC)


def attention_specs(length, seq, heads, sizes):
    first_rope = heads * NOPE // (2 * ROPE)
    whole = lambda shape: pl.BlockSpec(shape, lambda p: (0,) * len(shape))
    return [
        pl.BlockSpec((length, 2 * NOPE), lambda p: (0, p)),
        pl.BlockSpec((length, 2 * ROPE), lambda p: (0, first_rope + p)),
        whole((length, 2 * ROPE)),
        whole((length, 2 * ROPE)),
        pl.BlockSpec((seq, 2 * (NOPE + VDIM)), lambda p: (0, p)),
        whole((seq, 2 * ROPE)),
        whole((sizes[0], sizes[1], sizes[4])),
    ]


def attend(linear, tables, kv, kr, bias, heads):
    length, seq = linear.shape[0], kv.shape[0]
    sizes = attention_sizes(length, seq)
    return pl.pallas_call(
        functools.partial(attend_kernel, sizes),
        grid=(heads // 2,),
        in_specs=attention_specs(length, seq, heads, sizes),
        out_specs=pl.BlockSpec((length, 2 * VDIM), lambda p: (0, p)),
        out_shape=jax.ShapeDtypeStruct((length, heads * VDIM), bf16),
        compiler_params=pltpu.CompilerParams(vmem_limit_bytes=48 * MIB),
        cost_estimate=time_of(27),
        name="attend",
    )(linear, linear, *tables, kv, kr, bias)


def attend_back(linear, tables, kv, kr, bias, grad, heads):
    length, seq = linear.shape[0], kv.shape[0]
    sizes = attention_sizes(length, seq)
    return pl.pallas_call(
        functools.partial(attend_back_kernel, sizes),
        grid=(heads // 2,),
        in_specs=attention_specs(length, seq, heads, sizes)
        + [pl.BlockSpec((length, 2 * VDIM), lambda p: (0, p))],
        out_specs=[
            pl.BlockSpec((length, 2 * NOPE), lambda p: (0, p)),
            pl.BlockSpec((length, 2 * ROPE), lambda p: (0, p)),
            pl.BlockSpec((seq, 2 * (NOPE + VDIM)), lambda p: (0, p)),
            pl.BlockSpec((seq, 2 * ROPE), lambda p: (0, 0)),
        ],
        out_shape=[
            jax.ShapeDtypeStruct((length, heads * NOPE), bf16),
            jax.ShapeDtypeStruct((length, heads * ROPE), bf16),
            jax.ShapeDtypeStruct((seq, heads * (NOPE + VDIM)), bf16),
            jax.ShapeDtypeStruct((seq, 2 * ROPE), f32),
        ],
        scratch_shapes=[pltpu.VMEM((2, seq, NOPE), f32), pltpu.VMEM((2, seq, VDIM), f32)],
        compiler_params=pltpu.CompilerParams(vmem_limit_bytes=48 * MIB),
        cost_estimate=time_of(51),
        name="attend_back",
    )(linear, linear, *tables, kv, kr, bias, grad)


def one_hot(place_ref, slots):
    place = place_ref[0]
    slot = lax.broadcasted_iota(jnp.int32, (slots, place.shape[1]), 0)
    return slot == place


def width_parts(refs, width):
    step = width // len(refs)
    return [(ref, pl.ds(i * step, step)) for i, ref in enumerate(refs)]


def forward_kernel(n, slots, place_ref, rows_ref, *refs):
    weights, shared, outs = refs[:n], refs[n : 2 * n], refs[2 * n :]
    picked_ref, act_ref, up_slope_ref, silu_ref, act_s_ref, up_slope_s_ref, silu_s_ref = outs
    width = rows_ref.shape[-1]
    picks = one_hot(place_ref, slots).astype(f32).astype(bf16)
    picked_ref[0] = dot(picks, rows_ref[0], 1, 0).astype(bf16)
    both = total([dot(picked_ref[0, :, at], w[...], 1, 0) for w, at in width_parts(weights, width)])
    half = both.shape[1] // 2
    silu, slope = silu_parts(both[:, :half])
    up = both[:, half:]
    act_ref[0] = (silu * up).astype(bf16)
    up_slope_ref[0] = (up * slope).astype(bf16)
    silu_ref[0] = silu.astype(bf16)
    both = total([dot(rows_ref[0, :, at], w[...], 1, 0) for w, at in width_parts(shared, width)])
    half = both.shape[1] // 2
    silu, slope = silu_parts(both[:, :half])
    up = both[:, half:]
    act_s_ref[0] = (silu * up).astype(bf16)
    up_slope_s_ref[0] = (up * slope).astype(bf16)
    silu_s_ref[0] = silu.astype(bf16)


def hidden_kernel(
    n, slots, place_ref, weight_ref, grads_ref, us_ref, silu_ref, us_s_ref, silu_s_ref, *refs
):
    down, down_s = refs[:n], refs[n : 2 * n]
    picked_ref, d_gate_ref, d_up_ref, d_shared_ref = refs[2 * n :]
    width = grads_ref.shape[-1]
    hot = one_hot(place_ref, slots)
    slot_weight = jnp.sum(jnp.where(hot, weight_ref[0], 0.0), axis=1, keepdims=True)
    picks = hot.astype(f32).astype(bf16)
    picked_ref[0] = (dot(picks, grads_ref[0], 1, 0) * slot_weight).astype(bf16)
    d_act = total([dot(picked_ref[0, :, at], w[...], 1, 1) for w, at in width_parts(down, width)])
    d_gate_ref[0] = (d_act * us_ref[0].astype(f32)).astype(bf16)
    d_up_ref[0] = (d_act * silu_ref[0].astype(f32)).astype(bf16)
    d_act = total([dot(grads_ref[0, :, at], w[...], 1, 0) for w, at in width_parts(down_s, width)])
    half = d_act.shape[1]
    d_shared_ref[0, :, :half] = (d_act * us_s_ref[0].astype(f32)).astype(bf16)
    d_shared_ref[0, :, half:] = (d_act * silu_s_ref[0].astype(f32)).astype(bf16)


def rows_kernel(
    slots, place_ref, d_gate_ref, d_up_ref, d_shared_ref, gate_up_ref, gate_up_s_ref, d_rows_ref
):
    picks = one_hot(place_ref, slots).astype(f32).astype(bf16)
    d_both = jnp.concatenate([d_gate_ref[0], d_up_ref[0]], axis=1)
    d_row = dot(d_both, gate_up_ref[...], 1, 1).astype(bf16)
    d_rows_ref[0] = (
        dot(picks, d_row, 0, 0) + dot(d_shared_ref[0], gate_up_s_ref[...], 1, 1)
    ).astype(bf16)


def output_kernel(n, slots, place_ref, weight_ref, act_ref, act_s_ref, *refs):
    down, down_s, outs = refs[:n], refs[n : 2 * n], refs[2 * n :]
    hot = one_hot(place_ref, slots)
    slot_weight = jnp.sum(jnp.where(hot, weight_ref[0], 0.0), axis=1, keepdims=True)
    picks = hot.astype(f32).astype(bf16)
    bounds = [0, outs[0].shape[-1], outs[0].shape[-1] + outs[1].shape[-1]]
    for i, (w, w_s) in enumerate(zip(down, down_s)):
        out = (dot(act_ref[0], w[...], 1, 0) * slot_weight).astype(bf16)
        rows = (dot(picks, out, 0, 0) + dot(act_s_ref[0], w_s[...], 1, 1)).astype(bf16)
        first = i * w.shape[1]
        for out_ref, low, high in zip(outs, bounds, bounds[1:]):
            low_in, high_in = max(low, first), min(high, first + w.shape[1])
            if low_in < high_in:
                out_ref[0, :, low_in - low : high_in - low] = rows[:, low_in - first : high_in - first]


def by_block(kernel, name, blocked, fixed, outs, flops):
    count = blocked[0].shape[0]
    block = lambda a: pl.BlockSpec((1, *a.shape[1:]), lambda b: (b, 0, 0))
    stay = lambda a: pl.BlockSpec(a.shape, lambda b: (0, 0), pipeline_mode=pl.Buffered(1))
    moved = sum(a.size * a.dtype.itemsize for a in (*blocked, *fixed, *outs))
    return pl.pallas_call(
        kernel,
        grid=(count,),
        in_specs=[block(a) for a in blocked] + [stay(a) for a in fixed],
        out_specs=[block(a) for a in outs],
        out_shape=outs,
        compiler_params=pltpu.CompilerParams(vmem_limit_bytes=60 * MIB),
        cost_estimate=pl.CostEstimate(flops=flops, bytes_accessed=moved, transcendentals=0),
        name=name,
    )(*blocked, *fixed)


def neighbours():
    dp, expert = lax.axis_index("dp"), lax.axis_index("expert")
    core, y = expert % 2, (expert // 2) % 2
    z_low, z_high = (expert // 4) % 2, expert // 8
    partners = [
        {"expert": expert + 1 - 2 * core},
        {"dp": 1 - dp},
        {"expert": expert + 2 - 4 * y},
        {"expert": expert + 4 - 8 * z_low},
        {"expert": expert + 8 - 16 * z_high},
    ]
    barrier = pltpu.get_barrier_semaphore()
    for partner in partners:
        pl.semaphore_signal(barrier, inc=1, device_id=partner, device_id_type=pl.DeviceIdType.MESH)
    pl.semaphore_wait(barrier, len(partners))
    return partners, (core, dp, y, z_low, z_high)


PIECE = 64 * 1024


def chunks_of(shapes):
    chunks = []
    for i, (rows, columns) in enumerate(shapes):
        wide = min(columns, 1024)
        tall = rows
        while tall > 16 and tall * wide > PIECE:
            tall //= 2
        chunks += [
            (i, top, tall, left, min(wide, columns - left))
            for top in range(0, rows, tall)
            for left in range(0, columns, wide)
        ]
    return chunks


def piece_of(chunk):
    _, top, tall, left, wide = chunk
    return pl.ds(top, tall), pl.ds(left, wide)


def time_of(microseconds):
    return pl.CostEstimate(
        flops=0, bytes_accessed=int(microseconds * 3.69e6), transcendentals=0
    )


def gather_kernel(chunks, n, *refs):
    ins, outs = refs[:n], refs[n : 2 * n]
    own_sem, send_sem, recv_sem = refs[2 * n :]
    partners, (core, dp, y, z_low, z_high) = neighbours()
    mine = (dp, z_high, z_low, y, core)
    place = [4, 0, 3, 2, 1]
    own = [pltpu.make_async_copy(ins[i], outs[i].at[mine], own_sem.at[i]) for i in range(n)]
    for copy in own:
        copy.start()
    copies = {}
    waited = set()
    count = len(chunks)

    def order(k):
        return [4, 2, 3, 1, 0] if k % 2 else [4, 3, 2, 1, 0]

    for turn in range(count + 5):
        for stage in range(5):
            k = turn - stage
            if not 0 <= k < count:
                continue
            array = chunks[k][0]
            gathered = [place[axis] for axis in order(k)[:stage]]
            held = [slice(None) if d in gathered else mine[d] for d in range(5)]
            there = outs[array].at[(*held, *piece_of(chunks[k]))]
            if stage == 0:
                here = ins[array].at[piece_of(chunks[k])]
            else:
                here = there
                copies[stage - 1, k].wait_recv()
            if stage == 1 and array not in waited:
                waited.add(array)
                own[array].wait()
            copies[stage, k] = pltpu.make_async_remote_copy(
                src_ref=here,
                dst_ref=there,
                send_sem=send_sem.at[stage, k],
                recv_sem=recv_sem.at[stage, k],
                device_id=partners[order(k)[stage]],
                device_id_type=pl.DeviceIdType.MESH,
            )
            copies[stage, k].start()
    for k in range(count):
        copies[4, k].wait_recv()
    for copy in copies.values():
        copy.wait_send()


def gather_all(arrays):
    chunks = chunks_of([a.shape for a in arrays])
    dims = (2, 2, 2, 2, 2)
    n = len(arrays)
    gathered = pl.pallas_call(
        functools.partial(gather_kernel, chunks, n),
        in_specs=[pl.BlockSpec(memory_space=pl.ANY)] * n,
        out_specs=[pl.BlockSpec(memory_space=pl.ANY)] * n,
        out_shape=[jax.ShapeDtypeStruct((*dims, *a.shape), a.dtype) for a in arrays],
        scratch_shapes=[
            pltpu.SemaphoreType.DMA((n,)),
            pltpu.SemaphoreType.DMA((5, len(chunks))),
            pltpu.SemaphoreType.DMA((5, len(chunks))),
        ],
        compiler_params=pltpu.CompilerParams(collective_id=2, has_side_effects=True),
        cost_estimate=time_of(180),
        name="gather_all",
    )(*arrays)
    return [g.reshape(-1, a.shape[1]) for g, a in zip(gathered, arrays)]


def add_rows(into, left, right):
    step = 16
    lead = (slice(None),) * (len(into.shape) - 2)

    @pl.loop(0, into.shape[-2] // step)
    def _(i):
        at = (*lead, pl.ds(pl.multiple_of(i * step, step), step), slice(None))
        into[at] = (left[at].astype(f32) + right[at].astype(f32)).astype(into.dtype)


def grad_sum_kernel(chunks, n, *refs):
    ins, outs = refs[:n], refs[n : 2 * n]
    count = len(chunks)
    own = refs[2 * n : 2 * n + count]
    got = [refs[2 * n + (i + 1) * count :][:count] for i in range(5)]
    load_sem, send_sem, recv_sem = refs[-3:]
    partners, mine = neighbours()
    core = mine[0]

    def source(k, which):
        array = chunks[k][0]
        lead = (slice(None),) * (len(ins[array].shape) - 3)
        return ins[array].at[(*lead, which, *piece_of(chunks[k]))]

    def pick(ref, stage, which):
        lead = [0, 0, 2, 1, 0][stage]
        return ref.at[(*(slice(None),) * lead, which)]

    def stages(k):
        return [0, 1, 2, 3, 4] if len(ins[chunks[k][0]].shape) == 7 else [0, 2, 3, 4]

    copies = {}

    def start(stage, k, values):
        copies[stage, k] = pltpu.make_async_remote_copy(
            src_ref=values,
            dst_ref=got[stage][k],
            send_sem=send_sem.at[stage, k],
            recv_sem=recv_sem.at[stage, k],
            device_id=partners[stage],
            device_id_type=pl.DeviceIdType.MESH,
        )
        copies[stage, k].start()

    loads = [pltpu.make_async_copy(source(k, core), own[k], load_sem.at[k]) for k in range(count)]
    for k in range(count):
        start(0, k, source(k, 1 - core))
        loads[k].start()
    for turn in range(count + 4):
        for step in range(5):
            k = turn - step
            if not 0 <= k < count or step >= len(stages(k)):
                continue
            stage = stages(k)[step]
            later = stages(k)[step + 1] if step + 1 < len(stages(k)) else None
            held = got[stage][k]
            copies[stage, k].wait_recv()
            if step == 0:
                loads[k].wait()
                sent, kept = 1 - mine[later], mine[later]
                part = pick(held, later, sent)
                add_rows(part, part, pick(own[k], later, sent))
                start(later, k, part)
                part = pick(held, later, kept)
                add_rows(part, part, pick(own[k], later, kept))
                continue
            kept = pick(got[stages(k)[step - 1]][k], stage, mine[stage])
            if later is None:
                add_rows(outs[chunks[k][0]].at[piece_of(chunks[k])], held, kept)
            else:
                add_rows(held, held, kept)
                start(later, k, pick(held, later, 1 - mine[later]))
    for copy in copies.values():
        copy.wait_send()


def grad_sums(arrays, over_dp):
    n = len(arrays)
    dims = [(2,) * (5 if o else 4) for o in over_dp]
    rows = [a.shape[0] // 2 ** len(d) for a, d in zip(arrays, dims)]
    chunks = chunks_of([(r, a.shape[1]) for r, a in zip(rows, arrays)])
    wider = [c for c in chunks if over_dp[c[0]]]
    narrower = [c for c in chunks if not over_dp[c[0]]]
    chunks = []
    while wider or narrower:
        chunks += wider[:1] + narrower[:1]
        wider, narrower = wider[1:], narrower[1:]

    def buffers(stage):
        shapes = []
        for i, _, tall, _, wide in chunks:
            lead = dims[i][:-1] if stage == 0 else (2,) * (4 - stage)
            unused = stage == 1 and not over_dp[i]
            shapes.append(pltpu.VMEM((16, 128) if unused else (*lead, tall, wide), bf16))
        return shapes

    return pl.pallas_call(
        functools.partial(grad_sum_kernel, chunks, n),
        in_specs=[pl.BlockSpec(memory_space=pl.ANY)] * n,
        out_specs=[pl.BlockSpec(memory_space=pltpu.VMEM)] * n,
        out_shape=[jax.ShapeDtypeStruct((r, a.shape[1]), f32) for r, a in zip(rows, arrays)],
        scratch_shapes=[
            *buffers(0),
            *[buffer for stage in range(5) for buffer in buffers(stage)],
            pltpu.SemaphoreType.DMA((len(chunks),)),
            pltpu.SemaphoreType.DMA((5, len(chunks))),
            pltpu.SemaphoreType.DMA((5, len(chunks))),
        ],
        compiler_params=pltpu.CompilerParams(
            collective_id=1, has_side_effects=True, vmem_limit_bytes=56 * MIB
        ),
        cost_estimate=time_of(170),
        name="grad_sums",
    )(*[a.reshape(*d, r, a.shape[1]) for a, d, r in zip(arrays, dims, rows)])


def swap(values):
    return lax.ppermute(values, "dp", [(0, 1), (1, 0)])


def turned(values, dp_count):
    if dp_count != 2:
        return values
    half = values.shape[-1] // 2
    a, b = values[..., :half], values[..., half:]
    first = lax.axis_index("dp") == 0
    return jnp.concatenate([jnp.where(first, a, b), jnp.where(first, b, a)], axis=-1)


def weight_parts(values, axis, dp_count):
    if dp_count != 2:
        return [lax.all_gather(values, "dp", axis=axis, tiled=True)]
    return [values, swap(values)]


def scatter_dp(results, axis):
    if len(results) == 1:
        return lax.psum_scatter(
            results[0]().astype(bf16), "dp", scatter_dimension=axis, tiled=True
        ).astype(f32)
    sent = swap(results[1]().astype(bf16))
    return results[0]() + sent.astype(f32)


def total(terms):
    return functools.reduce(jnp.add, terms)


def heads_apart(values, heads):
    by_head = values.reshape(-1, heads, NOPE + ROPE)
    rows = values.shape[0]
    return jnp.concatenate(
        [by_head[..., :NOPE].reshape(rows, -1), by_head[..., NOPE:].reshape(rows, -1)], axis=1
    )


def heads_together(values, heads):
    rows = values.shape[0]
    nope = values[:, : heads * NOPE].reshape(rows, heads, NOPE)
    rope = values[:, heads * NOPE :].reshape(rows, heads, ROPE)
    return jnp.concatenate([nope, rope], axis=-1).reshape(rows, -1)


def local(
    tokens,
    segments,
    routes,
    combine,
    input_gain,
    query_weight,
    latent_weight,
    latent_gain,
    expand_weight,
    output_weight,
    middle_gain,
    shared_gate,
    shared_up,
    shared_down,
    expert_gate,
    expert_up,
    expert_down,
    cotangent,
):
    _, length, width = tokens.shape
    seq = segments.shape[1]
    top_k = routes.shape[2]
    dp_count = lax.axis_size("dp")
    groups = lax.axis_size("expert")
    shards = dp_count * groups
    both = ("dp", "expert")
    hidden_s = shared_gate.shape[1]
    part_s = hidden_s // groups
    slots = length * top_k * 4 // (groups * 3)
    offset = lax.axis_index("dp") * length
    query_width = query_weight.shape[1]
    heads = query_width // (NOPE + ROPE)
    rows_w = query_weight.shape[0]

    g1 = input_gain.shape[0]
    hits = routes[0][:, None, :] == jnp.arange(groups, dtype=jnp.int32)[None, :, None]
    dense = jnp.sum(jnp.where(hits, combine[0][:, None, :], 0.0), axis=-1)
    dense = jnp.where(jnp.any(hits, axis=-1), dense, -1.0)
    my_weights = lax.all_to_all(dense.T, "expert", split_axis=0, concat_axis=0, tiled=True)
    chosen = my_weights >= 0.0
    before = jnp.arange(length)[:, None] < jnp.arange(length)[None, :]
    place = mm("bt,ts->bs", chosen.astype(bf16), before.astype(bf16)).astype(jnp.int32)
    place = jnp.where(chosen, place, -1)
    place = place[:, None, :]
    row_weights = my_weights[:, None, :]

    linear_width = query_width + RANK + ROPE
    gains = jnp.stack([input_gain, middle_gain, jnp.pad(latent_gain, (0, g1 - latent_gain.size))])
    gains = jnp.pad(gains, ((0, 13), (0, -g1 % 128)))
    own_linear = jnp.concatenate([heads_apart(query_weight, heads), latent_weight], axis=1)
    own_linear = jnp.pad(own_linear, ((0, 0), (0, -linear_width % 128)))
    shares = [gains, own_linear, expand_weight.T, output_weight.T]
    if dp_count == 2 and groups == 16:
        gains, query_latent, expand_t, output_t = gather_all(shares)
    else:
        gains, query_latent, expand_t, output_t = [
            lax.all_gather(v, both, axis=0, tiled=True) for v in shares
        ]
    gains = gains.reshape(shards, 16, -1)
    first_gain = gains[:, 0, :g1].reshape(-1).astype(f32)
    second_gain = gains[:, 1, :g1].reshape(-1).astype(f32)
    latent_norm = gains[:, 2, : latent_gain.size].reshape(-1).astype(f32)

    shared_own = jnp.stack(
        [
            shared_gate.reshape(rows_w, groups, part_s),
            shared_up.reshape(rows_w, groups, part_s),
            shared_down.T.reshape(rows_w, groups, part_s),
        ],
        axis=1,
    ).transpose(2, 0, 1, 3)
    shared_own = after(shared_own, expand_t)
    shared_cols = shared_moved = lax.all_to_all(shared_own, "expert", split_axis=0, concat_axis=0, tiled=True)
    shared_cols = weight_parts(shared_cols.reshape(groups * rows_w, 3 * part_s), 0, dp_count)
    padded_s = -(-part_s // 128) * 128
    wide_s = [
        jnp.pad(c.reshape(-1, 3, part_s), ((0, 0), (0, 0), (0, padded_s - part_s)))
        for c in shared_cols
    ]
    gate_up_s = [c[:, :2].reshape(-1, 2 * padded_s) for c in wide_s]
    down_s_t = [c[:, 2] for c in wide_s]

    own_e = after((expert_gate[0], expert_up[0], expert_down[0]), query_latent)
    gate_up_e = weight_parts(jnp.concatenate(own_e[:2], axis=1), 0, dp_count)
    down_e = weight_parts(own_e[2], 1, dp_count)

    token_values = tokens[0].astype(f32)
    scale_one = lax.rsqrt(jnp.mean(token_values * token_values, axis=-1, keepdims=True) + epsilon)
    normed_one = token_values * scale_one
    normed_low = (normed_one * first_gain).astype(bf16)
    own_pos = offset + jnp.arange(length, dtype=jnp.int32)
    cosine, sine = rotary_tables(own_pos)
    tables = (
        jnp.concatenate([cosine] * 4, axis=1),
        jnp.concatenate([-sine, sine, -sine, sine], axis=1),
    )
    linear = mm("rd,dk->rk", normed_low, query_latent)
    latent_raw = linear[:, query_width : query_width + RANK]
    latent_scale = lax.rsqrt(jnp.mean(latent_raw * latent_raw, axis=-1, keepdims=True) + epsilon)
    latent_normed = latent_raw * latent_scale
    latent_low = (latent_normed * latent_norm).astype(bf16)
    rope_low = rotate(linear[:, query_width + RANK : linear_width], cosine, sine).astype(bf16)
    latent_rope = jnp.concatenate([latent_low, rope_low], axis=-1)
    if dp_count == 2:
        other = swap(latent_rope)
        is_first = lax.axis_index("dp") == 0
        latent_rope = jnp.concatenate(
            [jnp.where(is_first, latent_rope, other), jnp.where(is_first, other, latent_rope)]
        )
    else:
        latent_rope = lax.all_gather(latent_rope, "dp", axis=0, tiled=True)
    latent_all = latent_rope[:, :RANK]
    rope_keys = jnp.concatenate([latent_rope[:, RANK:]] * 2, axis=1)
    expanded = mm("rc,kc->rk", latent_all, expand_t).astype(bf16)
    blocks, block_rows, _, _, reach = attention_sizes(length, seq)
    bias = []
    for block in range(blocks):
        start = window_start(block, block_rows, length, seq, reach)
        q_pos = offset + block * block_rows + jnp.arange(block_rows)
        q_seg = lax.dynamic_slice_in_dim(segments[0], offset + block * block_rows, block_rows)
        k_seg = lax.dynamic_slice_in_dim(segments[0], start, reach)
        seen = (q_seg[:, None] == k_seg[None, :]) & (
            q_pos[:, None] >= (start + jnp.arange(reach))[None, :]
        )
        bias.append(jnp.where(seen, 0.0, -1e30).astype(f32))
    bias = jnp.stack(bias)
    mixed = attend(linear, tables, expanded, rope_keys, bias, heads)
    middle = token_values + mm("rv,dv->rd", mixed, output_t)
    scale_two = lax.rsqrt(jnp.mean(middle * middle, axis=-1, keepdims=True) + epsilon)
    normed_two = middle * scale_two
    ffn_rows = (normed_two * second_gain).astype(bf16)

    def gather_rows(values):
        return lax.all_gather(values, "expert", axis=0, tiled=False)

    grads_all = gather_rows(turned(cotangent[0], dp_count))
    rows_all = gather_rows(
        after(turned(ffn_rows, dp_count), (grads_all, shared_moved, my_weights))
    )

    def flat(values):
        return values.reshape(-1, values.shape[-1])

    def scatter_rows(values):
        return lax.psum_scatter(flat(values), "expert", scatter_dimension=0, tiled=True)

    n = len(gate_up_e)
    hidden = expert_gate.shape[2]
    block_of = lambda rows, columns: jax.ShapeDtypeStruct((groups, rows, columns), bf16)
    wide = [block_of(slots, hidden)] * 3
    wide_shared = [block_of(length, padded_s)] * 3
    aside = 3 * width // 16
    unit = 2 * groups * width
    picked, act_e, up_slope, silu, act_s, up_slope_s, silu_s = by_block(
        functools.partial(forward_kernel, n, slots),
        "experts_forward",
        [place, rows_all],
        [*gate_up_e, *gate_up_s],
        [block_of(slots, width), *wide, *wide_shared],
        unit * (slots * (length + 2 * hidden) + 2 * length * padded_s),
    )
    picked_grad, d_gate, d_up, d_shared = by_block(
        functools.partial(hidden_kernel, n, slots),
        "experts_hidden",
        [place, row_weights, grads_all, up_slope, silu, up_slope_s, silu_s],
        [*down_e, *down_s_t],
        [block_of(slots, width), *wide[:2], block_of(length, 2 * padded_s)],
        unit * (slots * (length + hidden) + length * padded_s),
    )
    d_rows = []
    for weights, weights_s in zip(gate_up_e, gate_up_s):
        [part] = by_block(
            functools.partial(rows_kernel, slots),
            "experts_rows",
            [place, d_gate, d_up, d_shared if not d_rows else after(d_shared, part)],
            [weights, weights_s],
            [block_of(length, width // n)],
            unit // n * (slots * (length + 2 * hidden) + 2 * length * padded_s),
        )
        d_rows.append(scatter_rows(part))
    out_parts = by_block(
        functools.partial(output_kernel, n, slots),
        "experts_output",
        [place, row_weights, act_e, act_s],
        [*down_e, *down_s_t],
        [block_of(length, width - aside), block_of(length, aside)],
        unit * (slots * (length + hidden) + length * padded_s),
    )

    column_parts = lambda values: jnp.split(flat(values), n, axis=1)
    picked, picked_grad, rows_parts, grads_parts = map(
        column_parts, (picked, picked_grad, rows_all, grads_all)
    )
    act_e, act_s, d_gate, d_up, d_shared = map(flat, (act_e, act_s, d_gate, d_up, d_shared))
    grad_gate_e = scatter_dp([lambda p=p: mm("rd,rf->df", p, d_gate) for p in picked], 0)
    grad_up_e = scatter_dp([lambda p=p: mm("rd,rf->df", p, d_up) for p in picked], 0)
    grad_down_e = scatter_dp([lambda p=p: mm("rf,rd->fd", act_e, p) for p in picked_grad], 1)
    grad_s = scatter_dp(
        [
            lambda r=r, g=g: jnp.concatenate(
                [mm("rd,rf->df", r, d_shared), mm("rd,rf->df", g, act_s)], axis=1
            )
            for r, g in zip(rows_parts, grads_parts)
        ],
        0,
    )
    grad_s = grad_s.reshape(groups, rows_w, 3, padded_s)[..., :part_s].astype(bf16)
    d_rows, grad_gate_e, grad_up_e, grad_down_e, grad_s, out_parts = lax.optimization_barrier(
        (d_rows, grad_gate_e, grad_up_e, grad_down_e, grad_s, out_parts)
    )
    grad_s = lax.all_to_all(grad_s, "expert", split_axis=0, concat_axis=0, tiled=True)
    grad_s = grad_s.transpose(2, 1, 0, 3).reshape(3, rows_w, hidden_s).astype(f32)
    d_rows_own = turned(jnp.concatenate(d_rows, axis=1), dp_count).astype(f32)

    out_grad = cotangent[0].astype(f32)
    middle_part, second_gain_grad = norm_back(d_rows_own, normed_two, scale_two, second_gain)
    middle_grad = out_grad + middle_part
    attn_grad = middle_grad.astype(bf16)
    mixed_grad = mm("rd,dv->rv", attn_grad, output_t).astype(bf16)
    attn_parts = jnp.split(turned(attn_grad, dp_count), n, axis=1)
    early = mixed.shape[1] // 2
    grad_out_t = [lambda p=p: mm("rd,rv->dv", p, mixed[:, :early]) for p in attn_parts]
    if dp_count == 2:
        sent, mixed_grad = lax.optimization_barrier((grad_out_t[1]().astype(bf16), mixed_grad))
        grad_out_t = grad_out_t[0]() + swap(sent).astype(f32)
    else:
        grad_out_t = scatter_dp(grad_out_t, 0)
    grad_out_t = [grad_out_t.astype(bf16), mm("rd,rv->dv", attn_grad, mixed[:, early:]).astype(bf16)]
    out_sum = scatter_rows(after(out_parts[0], d_rows))
    d_nope, d_rope, d_expanded, d_keys_rope = attend_back(
        linear, tables, expanded, rope_keys, bias, mixed_grad, heads
    )
    d_expanded, grad_out_t[0] = lax.optimization_barrier((d_expanded, grad_out_t[0]))
    latent_part = mm("rk,kc->rc", d_expanded, expand_t)
    rope_part = d_keys_rope[:, :ROPE] + d_keys_rope[:, ROPE:]
    latent_rope_part = jnp.concatenate([latent_part, rope_part], axis=-1)
    if dp_count == 2:
        first_half, second_half = latent_rope_part[:length], latent_rope_part[length:]
        is_first = lax.axis_index("dp") == 0
        sent = swap(jnp.where(is_first, second_half, first_half).astype(bf16))
        combined = jnp.where(is_first, first_half, second_half) + sent.astype(f32)
    else:
        combined = lax.psum_scatter(latent_rope_part, "dp", scatter_dimension=0, tiled=True)
    grad_expand_t = mm("rk,rc->kc", d_expanded, latent_all).astype(bf16)
    latent_grad, latent_gain_grad = norm_back(
        combined[:, :RANK], latent_normed, latent_scale, latent_norm
    )
    rope_grad = rotate_back(combined[:, RANK:], cosine, sine)
    linear_grad = jnp.concatenate(
        [d_nope, d_rope, latent_grad.astype(bf16), rope_grad.astype(bf16)], axis=-1
    )
    linear_grad = jnp.pad(linear_grad, ((0, 0), (0, -linear_width % 128)))
    normed_grad = mm("rk,dk->rd", linear_grad, query_latent)
    input_part, first_gain_grad = norm_back(normed_grad, normed_one, scale_one, first_gain)
    tokens_grad = (middle_grad + input_part)[None]
    small = jnp.stack(
        [
            first_gain_grad,
            second_gain_grad,
            jnp.pad(
                latent_gain_grad.reshape(shards, -1), ((0, 0), (0, g1 - RANK // shards))
            ).reshape(-1),
        ],
        axis=1,
    )
    small = jnp.pad(small, ((0, 0), (0, -small.shape[1] % 128))).astype(bf16)
    grad_linear = mm("rd,rk->dk", normed_low, linear_grad).astype(bf16)
    sums = [*grad_out_t, flat(out_parts[1]), grad_expand_t, grad_linear, small]
    over_dp = [False, True, False, True, True, True]
    if dp_count == 2 and groups == 16:
        sums = grad_sums(sums, over_dp)
    else:
        sums = [
            lax.psum_scatter(v, both if o else "expert", scatter_dimension=0, tiled=True)
            for v, o in zip(sums, over_dp)
        ]
        sums = [v.astype(f32) for v in sums]
    *grad_out_t, out_aside, grad_expand_t, grad_linear, small = sums
    out_sum = after(out_sum, grad_linear)
    out_sum = jnp.concatenate([out_sum.astype(f32), out_aside], axis=1)
    outputs = (middle + turned(out_sum, dp_count)).astype(bf16)[None]
    return (
        outputs,
        tokens_grad,
        small[:, 0],
        heads_together(grad_linear[:, :query_width], heads),
        grad_linear[:, query_width:linear_width],
        small[: RANK // shards, 2],
        grad_expand_t.T,
        jnp.concatenate(grad_out_t, axis=1).T,
        small[:, 1],
        grad_s[0],
        grad_s[1],
        grad_s[2].T,
        grad_gate_e[None],
        grad_up_e[None],
        grad_down_e[None],
    )


def solution(mesh):
    rows = P("expert", "dp", None)
    first = P(("dp", "expert"), None)
    last = P(None, ("dp", "expert"))
    vector = P(("dp", "expert"))
    down = P("expert", None, "dp")
    return jax.shard_map(
        local,
        mesh=mesh,
        in_specs=(
            rows,
            P("expert", None),
            rows,
            rows,
            vector,
            first,
            first,
            vector,
            last,
            last,
            vector,
            first,
            first,
            last,
            rows,
            rows,
            down,
            rows,
        ),
        out_specs=(
            rows,
            rows,
            vector,
            first,
            first,
            vector,
            last,
            last,
            vector,
            first,
            first,
            last,
            rows,
            rows,
            down,
        ),
        check_vma=False,
    )
```

```python
import functools

import jax
import jax.numpy as jnp
from jax import lax
from jax.experimental import pallas as pl
from jax.experimental.pallas import tpu as pltpu
from jax.sharding import PartitionSpec as P

NOPE = 128
ROPE = 64
VDIM = 128
RANK = 512
DOC = 512
epsilon = 1e-06
f32 = jnp.float32
bf16 = jnp.bfloat16
MIB = 1 << 20
TILE = 256


def mm(spec, a, b):
    return jnp.einsum(spec, a, b, preferred_element_type=f32)


def dot(a, b, ca, cb):
    return lax.dot_general(a, b, (((ca,), (cb,)), ((), ())), preferred_element_type=f32)


def after(values, earlier):
    return lax.optimization_barrier((values, earlier))[0]


def rotate(values, cosine, sine):
    half = values.shape[-1] // 2
    a, b = values[..., :half], values[..., half:]
    return jnp.concatenate([a * cosine - b * sine, b * cosine + a * sine], axis=-1)


def rotate_back(values, cosine, sine):
    return rotate(values, cosine, -sine)


def norm_back(gradient, normed, scale_vec, gain_vec):
    scaled = gradient * gain_vec
    inner = jnp.mean(scaled * normed, axis=-1, keepdims=True)
    return scale_vec * (scaled - normed * inner), jnp.sum(gradient * normed, axis=0)


def silu_parts(gate_in):
    sig = jax.nn.sigmoid(gate_in)
    return gate_in * sig, sig * (1.0 + gate_in * (1.0 - sig))


def rotary_tables(positions):
    frequency = jnp.power(10000.0, -jnp.arange(ROPE // 2).astype(f32) * 2.0 / ROPE)
    angles = positions.astype(f32)[:, None] * frequency[None, :]
    return jnp.cos(angles), jnp.sin(angles)


def window_start(block, rows, length, seq, reach):
    first = lax.axis_index("dp") * length + block * rows - DOC
    return jnp.clip(first, 0, seq - reach)


def swap_halves(values):
    lane = lax.broadcasted_iota(jnp.int32, values.shape, 1)
    up = pltpu.roll(values, ROPE // 2, 1)
    down = pltpu.roll(values, 2 * ROPE - ROPE // 2, 1)
    return jnp.where(lane % ROPE < ROPE // 2, down, up)


def head_lanes(shape, head):
    lane = lax.broadcasted_iota(jnp.int32, shape, 1)
    return (lane // ROPE) == head


def probabilities(q, qr, k, kr, bias):
    scores = (dot(q, k, 1, 1) + dot(qr, kr, 1, 1)) * (NOPE + ROPE) ** (-0.5) + bias
    exponent = jnp.exp(scores - jnp.max(scores, axis=-1, keepdims=True))
    return exponent / jnp.sum(exponent, axis=-1, keepdims=True)


def attend_kernel(sizes, nope_ref, rope_ref, cos_ref, sin_ref, kv_ref, kr_ref, bias_ref, out_ref):
    blocks, rows, length, seq, reach = sizes
    for block in range(blocks):
        at = pl.ds(block * rows, rows)
        rope = rope_ref[at, :]
        rope = (rope * cos_ref[at, :] + swap_halves(rope) * sin_ref[at, :]).astype(bf16)
        start = pl.multiple_of(window_start(block, rows, length, seq, reach), 128)
        span = pl.ds(start, reach)
        kr = kr_ref[span, :]
        for head in range(2):
            qr = jnp.where(head_lanes(rope.shape, head), rope, jnp.zeros_like(rope))
            q = nope_ref[at, head * NOPE : (head + 1) * NOPE].astype(bf16)
            k = kv_ref[span, head * 256 : head * 256 + NOPE]
            v = kv_ref[span, head * 256 + NOPE : (head + 1) * 256]
            probs = probabilities(q, qr, k, kr, bias_ref[block])
            out_ref[at, head * VDIM : (head + 1) * VDIM] = dot(
                probs.astype(bf16), v, 1, 0
            ).astype(bf16)


def attend_back_kernel(
    sizes,
    nope_ref,
    rope_ref,
    cos_ref,
    sin_ref,
    kv_ref,
    kr_ref,
    bias_ref,
    grad_ref,
    dnope_ref,
    drope_ref,
    dkv_ref,
    dkr_ref,
    dk_acc,
    dv_acc,
):
    blocks, rows, length, seq, reach = sizes
    factor = (NOPE + ROPE) ** (-0.5)

    @pl.when(pl.program_id(0) == 0)
    def _():
        dkr_ref[...] = jnp.zeros_like(dkr_ref)

    dk_acc[...] = jnp.zeros_like(dk_acc)
    dv_acc[...] = jnp.zeros_like(dv_acc)
    for block in range(blocks):
        at = pl.ds(block * rows, rows)
        rope = rope_ref[at, :]
        rope = (rope * cos_ref[at, :] + swap_halves(rope) * sin_ref[at, :]).astype(bf16)
        start = pl.multiple_of(window_start(block, rows, length, seq, reach), 128)
        span = pl.ds(start, reach)
        kr = kr_ref[span, :]
        rope_grad = jnp.zeros((rows, 2 * ROPE), f32)
        for head in range(2):
            mine = head_lanes(rope.shape, head)
            qr = jnp.where(mine, rope, jnp.zeros_like(rope))
            q = nope_ref[at, head * NOPE : (head + 1) * NOPE].astype(bf16)
            k = kv_ref[span, head * 256 : head * 256 + NOPE]
            v = kv_ref[span, head * 256 + NOPE : (head + 1) * 256]
            grad = grad_ref[at, head * VDIM : (head + 1) * VDIM]
            probs = probabilities(q, qr, k, kr, bias_ref[block])
            dprobs = dot(grad, v, 1, 1)
            inner = jnp.sum(dprobs * probs, axis=-1, keepdims=True)
            dscores = (probs * (dprobs - inner) * factor).astype(bf16)
            dnope_ref[at, head * NOPE : (head + 1) * NOPE] = dot(dscores, k, 1, 0).astype(bf16)
            rope_grad += jnp.where(mine, dot(dscores, kr, 1, 0), 0.0)
            dk_acc[head, span, :] += dot(dscores, q, 0, 0)
            dv_acc[head, span, :] += dot(probs.astype(bf16), grad, 0, 0)
            dkr_ref[span, :] += dot(dscores, qr, 0, 0)
        rope_grad = rope_grad * cos_ref[at, :] - swap_halves(rope_grad) * sin_ref[at, :]
        drope_ref[at, :] = rope_grad.astype(bf16)
    for head in range(2):
        dkv_ref[:, head * 256 : head * 256 + NOPE] = dk_acc[head].astype(bf16)
        dkv_ref[:, head * 256 + NOPE : (head + 1) * 256] = dv_acc[head].astype(bf16)


def attention_sizes(length, seq):
    rows = min(256, length)
    return length // rows, rows, length, seq, min(seq, rows + DOC)


def attention_specs(length, seq, heads, sizes):
    first_rope = heads * NOPE // (2 * ROPE)
    whole = lambda shape: pl.BlockSpec(shape, lambda p: (0,) * len(shape))
    return [
        pl.BlockSpec((length, 2 * NOPE), lambda p: (0, p)),
        pl.BlockSpec((length, 2 * ROPE), lambda p: (0, first_rope + p)),
        whole((length, 2 * ROPE)),
        whole((length, 2 * ROPE)),
        pl.BlockSpec((seq, 2 * (NOPE + VDIM)), lambda p: (0, p)),
        whole((seq, 2 * ROPE)),
        whole((sizes[0], sizes[1], sizes[4])),
    ]


def attend(linear, tables, kv, kr, bias, heads):
    length, seq = linear.shape[0], kv.shape[0]
    sizes = attention_sizes(length, seq)
    return pl.pallas_call(
        functools.partial(attend_kernel, sizes),
        grid=(heads // 2,),
        in_specs=attention_specs(length, seq, heads, sizes),
        out_specs=pl.BlockSpec((length, 2 * VDIM), lambda p: (0, p)),
        out_shape=jax.ShapeDtypeStruct((length, heads * VDIM), bf16),
        compiler_params=pltpu.CompilerParams(vmem_limit_bytes=48 * MIB),
        cost_estimate=time_of(27),
        name="attend",
    )(linear, linear, *tables, kv, kr, bias)


def attend_back(linear, tables, kv, kr, bias, grad, heads):
    length, seq = linear.shape[0], kv.shape[0]
    sizes = attention_sizes(length, seq)
    return pl.pallas_call(
        functools.partial(attend_back_kernel, sizes),
        grid=(heads // 2,),
        in_specs=attention_specs(length, seq, heads, sizes)
        + [pl.BlockSpec((length, 2 * VDIM), lambda p: (0, p))],
        out_specs=[
            pl.BlockSpec((length, 2 * NOPE), lambda p: (0, p)),
            pl.BlockSpec((length, 2 * ROPE), lambda p: (0, p)),
            pl.BlockSpec((seq, 2 * (NOPE + VDIM)), lambda p: (0, p)),
            pl.BlockSpec((seq, 2 * ROPE), lambda p: (0, 0)),
        ],
        out_shape=[
            jax.ShapeDtypeStruct((length, heads * NOPE), bf16),
            jax.ShapeDtypeStruct((length, heads * ROPE), bf16),
            jax.ShapeDtypeStruct((seq, heads * (NOPE + VDIM)), bf16),
            jax.ShapeDtypeStruct((seq, 2 * ROPE), f32),
        ],
        scratch_shapes=[pltpu.VMEM((2, seq, NOPE), f32), pltpu.VMEM((2, seq, VDIM), f32)],
        compiler_params=pltpu.CompilerParams(vmem_limit_bytes=48 * MIB),
        cost_estimate=time_of(51),
        name="attend_back",
    )(linear, linear, *tables, kv, kr, bias, grad)


def one_hot(place_ref, slots):
    place = place_ref[0]
    slot = lax.broadcasted_iota(jnp.int32, (slots, place.shape[1]), 0)
    return slot == place


def width_parts(refs, width):
    step = width // len(refs)
    return [(ref, pl.ds(i * step, step)) for i, ref in enumerate(refs)]


def hidden_kernel(n, slots, place_ref, weight_ref, grads_ref, *refs):
    down, (picked_ref, d_act_ref) = refs[:n], refs[n:]
    width = grads_ref.shape[-1]
    hot = one_hot(place_ref, slots)
    slot_weight = jnp.sum(jnp.where(hot, weight_ref[0], 0.0), axis=1, keepdims=True)
    picks = hot.astype(f32).astype(bf16)
    picked_ref[0] = (dot(picks, grads_ref[0], 1, 0) * slot_weight).astype(bf16)
    d_act = total([dot(picked_ref[0, :, at], w[...], 1, 1) for w, at in width_parts(down, width)])
    d_act_ref[0] = d_act.astype(bf16)


def gated_tiles(values_ref, weights, d_act, act_ref, d_gate_ref, d_up_ref, up_first):
    width, hidden = values_ref.shape[-1], act_ref.shape[-1]
    for left in range(0, hidden, TILE):
        wide = min(TILE, hidden - left)
        here, above = pl.ds(left, wide), pl.ds(hidden + left, wide)
        parts = width_parts(weights, width)
        gate = total([dot(values_ref[0, :, at], w[:, here], 1, 0) for w, at in parts])
        up = total([dot(values_ref[0, :, at], w[:, above], 1, 0) for w, at in parts])
        silu, slope = silu_parts(gate)
        d_tile = d_act[:, left : left + wide].astype(f32)
        act_ref[0, :, here] = (silu * up).astype(bf16)
        d_gate_ref[0, :, here] = (d_tile * up * slope).astype(bf16)
        d_up_ref[0, :, pl.ds(up_first + left, wide)] = (d_tile * silu).astype(bf16)


def forward_kernel(n, slots, place_ref, rows_ref, grads_ref, d_act_ref, *refs):
    weights, shared, down_s, outs = refs[:n], refs[n : 2 * n], refs[2 * n : 3 * n], refs[3 * n :]
    picked_ref, act_ref, d_gate_ref, d_up_ref, act_s_ref, d_shared_ref = outs
    picks = one_hot(place_ref, slots).astype(f32).astype(bf16)
    picked_ref[0] = dot(picks, rows_ref[0], 1, 0).astype(bf16)
    gated_tiles(picked_ref, weights, d_act_ref.at[0], act_ref, d_gate_ref, d_up_ref, 0)
    half = act_s_ref.shape[-1]
    parts = width_parts(down_s, rows_ref.shape[-1])
    d_act_s = total([dot(grads_ref[0, :, at], w[...], 1, 0) for w, at in parts])
    gated_tiles(rows_ref, shared, d_act_s, act_s_ref, d_shared_ref, d_shared_ref, half)


def rows_kernel(
    slots, place_ref, d_gate_ref, d_up_ref, d_shared_ref, gate_up_ref, gate_up_s_ref, d_rows_ref
):
    picks = one_hot(place_ref, slots).astype(f32).astype(bf16)
    d_both = jnp.concatenate([d_gate_ref[0], d_up_ref[0]], axis=1)
    d_row = dot(d_both, gate_up_ref[...], 1, 1).astype(bf16)
    d_rows_ref[0] = (
        dot(picks, d_row, 0, 0) + dot(d_shared_ref[0], gate_up_s_ref[...], 1, 1)
    ).astype(bf16)


def output_kernel(n, slots, place_ref, weight_ref, act_ref, act_s_ref, *refs):
    down, down_s, outs = refs[:n], refs[n : 2 * n], refs[2 * n :]
    hot = one_hot(place_ref, slots)
    slot_weight = jnp.sum(jnp.where(hot, weight_ref[0], 0.0), axis=1, keepdims=True)
    picks = hot.astype(f32).astype(bf16)
    bounds = [0, outs[0].shape[-1], outs[0].shape[-1] + outs[1].shape[-1]]
    for i, (w, w_s) in enumerate(zip(down, down_s)):
        out = (dot(act_ref[0], w[...], 1, 0) * slot_weight).astype(bf16)
        rows = (dot(picks, out, 0, 0) + dot(act_s_ref[0], w_s[...], 1, 1)).astype(bf16)
        first = i * w.shape[1]
        for out_ref, low, high in zip(outs, bounds, bounds[1:]):
            low_in, high_in = max(low, first), min(high, first + w.shape[1])
            if low_in < high_in:
                out_ref[0, :, low_in - low : high_in - low] = rows[:, low_in - first : high_in - first]


def by_block(kernel, name, blocked, fixed, outs, flops):
    count = blocked[0].shape[0]
    block = lambda a: pl.BlockSpec((1, *a.shape[1:]), lambda b: (b, 0, 0))
    stay = lambda a: pl.BlockSpec(a.shape, lambda b: (0, 0), pipeline_mode=pl.Buffered(1))
    moved = sum(a.size * a.dtype.itemsize for a in (*blocked, *fixed, *outs))
    return pl.pallas_call(
        kernel,
        grid=(count,),
        in_specs=[block(a) for a in blocked] + [stay(a) for a in fixed],
        out_specs=[block(a) for a in outs],
        out_shape=outs,
        compiler_params=pltpu.CompilerParams(vmem_limit_bytes=60 * MIB),
        cost_estimate=pl.CostEstimate(flops=flops, bytes_accessed=moved, transcendentals=0),
        name=name,
    )(*blocked, *fixed)


def neighbours():
    dp, expert = lax.axis_index("dp"), lax.axis_index("expert")
    core, y = expert % 2, (expert // 2) % 2
    z_low, z_high = (expert // 4) % 2, expert // 8
    partners = [
        {"expert": expert + 1 - 2 * core},
        {"dp": 1 - dp},
        {"expert": expert + 2 - 4 * y},
        {"expert": expert + 4 - 8 * z_low},
        {"expert": expert + 8 - 16 * z_high},
    ]
    barrier = pltpu.get_barrier_semaphore()
    for partner in partners:
        pl.semaphore_signal(barrier, inc=1, device_id=partner, device_id_type=pl.DeviceIdType.MESH)
    pl.semaphore_wait(barrier, len(partners))
    return partners, (core, dp, y, z_low, z_high)


PIECE = 64 * 1024


def chunks_of(shapes):
    chunks = []
    for i, (rows, columns) in enumerate(shapes):
        wide = min(columns, 1024)
        tall = rows
        while tall > 16 and tall * wide > PIECE:
            tall //= 2
        chunks += [
            (i, top, tall, left, min(wide, columns - left))
            for top in range(0, rows, tall)
            for left in range(0, columns, wide)
        ]
    return chunks


def piece_of(chunk):
    _, top, tall, left, wide = chunk
    return pl.ds(top, tall), pl.ds(left, wide)


def time_of(microseconds):
    return pl.CostEstimate(
        flops=0, bytes_accessed=int(microseconds * 3.69e6), transcendentals=0
    )


def gather_kernel(chunks, n, *refs):
    ins, outs = refs[:n], refs[n + 1 : 2 * n + 1]
    own_sem, send_sem, recv_sem, cross_sem = refs[2 * n + 2 :]
    partners, (core, dp, y, z_low, z_high) = neighbours()
    crossing = pltpu.make_async_remote_copy(
        src_ref=refs[n],
        dst_ref=refs[2 * n + 1],
        send_sem=cross_sem.at[0],
        recv_sem=cross_sem.at[1],
        device_id=partners[1],
        device_id_type=pl.DeviceIdType.MESH,
    )
    crossing.start()
    mine = (dp, z_high, z_low, y, core)
    place = [4, 0, 3, 2, 1]
    own = [pltpu.make_async_copy(ins[i], outs[i].at[mine], own_sem.at[i]) for i in range(n)]
    for copy in own:
        copy.start()
    copies = {}
    waited = set()
    count = len(chunks)

    def order(k):
        return [4, 2, 3, 1, 0] if k % 2 else [4, 3, 2, 1, 0]

    for turn in range(count + 5):
        for stage in range(5):
            k = turn - stage
            if not 0 <= k < count:
                continue
            array = chunks[k][0]
            gathered = [place[axis] for axis in order(k)[:stage]]
            held = [slice(None) if d in gathered else mine[d] for d in range(5)]
            there = outs[array].at[(*held, *piece_of(chunks[k]))]
            if stage == 0:
                here = ins[array].at[piece_of(chunks[k])]
            else:
                here = there
                copies[stage - 1, k].wait_recv()
            if stage == 1 and array not in waited:
                waited.add(array)
                own[array].wait()
            copies[stage, k] = pltpu.make_async_remote_copy(
                src_ref=here,
                dst_ref=there,
                send_sem=send_sem.at[stage, k],
                recv_sem=recv_sem.at[stage, k],
                device_id=partners[order(k)[stage]],
                device_id_type=pl.DeviceIdType.MESH,
            )
            copies[stage, k].start()
    for k in range(count):
        copies[4, k].wait_recv()
    for copy in copies.values():
        copy.wait_send()
    crossing.wait()


def gather_all(arrays, crossed):
    chunks = chunks_of([a.shape for a in arrays])
    dims = (2, 2, 2, 2, 2)
    n = len(arrays)
    *gathered, crossed = pl.pallas_call(
        functools.partial(gather_kernel, chunks, n),
        in_specs=[pl.BlockSpec(memory_space=pl.ANY)] * (n + 1),
        out_specs=[pl.BlockSpec(memory_space=pl.ANY)] * (n + 1),
        out_shape=[
            *[jax.ShapeDtypeStruct((*dims, *a.shape), a.dtype) for a in arrays],
            jax.ShapeDtypeStruct(crossed.shape, crossed.dtype),
        ],
        scratch_shapes=[
            pltpu.SemaphoreType.DMA((n,)),
            pltpu.SemaphoreType.DMA((5, len(chunks))),
            pltpu.SemaphoreType.DMA((5, len(chunks))),
            pltpu.SemaphoreType.DMA((2,)),
        ],
        compiler_params=pltpu.CompilerParams(collective_id=2, has_side_effects=True),
        cost_estimate=time_of(180),
        name="gather_all",
    )(*arrays, crossed)
    return [g.reshape(-1, a.shape[1]) for g, a in zip(gathered, arrays)], crossed


def add_rows(into, left, right):
    step = 16
    lead = (slice(None),) * (len(into.shape) - 2)

    @pl.loop(0, into.shape[-2] // step)
    def _(i):
        at = (*lead, pl.ds(pl.multiple_of(i * step, step), step), slice(None))
        into[at] = (left[at].astype(f32) + right[at].astype(f32)).astype(into.dtype)


def grad_sum_kernel(chunks, n, *refs):
    ins, outs = refs[:n], refs[n : 2 * n]
    count = len(chunks)
    own = refs[2 * n : 2 * n + count]
    got = [refs[2 * n + (i + 1) * count :][:count] for i in range(5)]
    load_sem, send_sem, recv_sem = refs[-3:]
    partners, mine = neighbours()
    core = mine[0]

    def source(k, which):
        array = chunks[k][0]
        lead = (slice(None),) * (len(ins[array].shape) - 3)
        return ins[array].at[(*lead, which, *piece_of(chunks[k]))]

    def pick(ref, stage, which):
        lead = [0, 0, 2, 1, 0][stage]
        return ref.at[(*(slice(None),) * lead, which)]

    def stages(k):
        return [0, 1, 2, 3, 4] if len(ins[chunks[k][0]].shape) == 7 else [0, 2, 3, 4]

    copies = {}

    def start(stage, k, values):
        copies[stage, k] = pltpu.make_async_remote_copy(
            src_ref=values,
            dst_ref=got[stage][k],
            send_sem=send_sem.at[stage, k],
            recv_sem=recv_sem.at[stage, k],
            device_id=partners[stage],
            device_id_type=pl.DeviceIdType.MESH,
        )
        copies[stage, k].start()

    loads = [pltpu.make_async_copy(source(k, core), own[k], load_sem.at[k]) for k in range(count)]
    for k in range(count):
        start(0, k, source(k, 1 - core))
        loads[k].start()
    for turn in range(count + 4):
        for step in range(5):
            k = turn - step
            if not 0 <= k < count or step >= len(stages(k)):
                continue
            stage = stages(k)[step]
            later = stages(k)[step + 1] if step + 1 < len(stages(k)) else None
            held = got[stage][k]
            copies[stage, k].wait_recv()
            if step == 0:
                loads[k].wait()
                sent, kept = 1 - mine[later], mine[later]
                part = pick(held, later, sent)
                add_rows(part, part, pick(own[k], later, sent))
                start(later, k, part)
                part = pick(held, later, kept)
                add_rows(part, part, pick(own[k], later, kept))
                continue
            kept = pick(got[stages(k)[step - 1]][k], stage, mine[stage])
            if later is None:
                add_rows(outs[chunks[k][0]].at[piece_of(chunks[k])], held, kept)
            else:
                add_rows(held, held, kept)
                start(later, k, pick(held, later, 1 - mine[later]))
    for copy in copies.values():
        copy.wait_send()


def grad_sums(arrays, over_dp):
    n = len(arrays)
    dims = [(2,) * (5 if o else 4) for o in over_dp]
    rows = [a.shape[0] // 2 ** len(d) for a, d in zip(arrays, dims)]
    chunks = chunks_of([(r, a.shape[1]) for r, a in zip(rows, arrays)])
    wider = [c for c in chunks if over_dp[c[0]]]
    narrower = [c for c in chunks if not over_dp[c[0]]]
    chunks = []
    while wider or narrower:
        chunks += wider[:1] + narrower[:1]
        wider, narrower = wider[1:], narrower[1:]

    def buffers(stage):
        shapes = []
        for i, _, tall, _, wide in chunks:
            lead = dims[i][:-1] if stage == 0 else (2,) * (4 - stage)
            unused = stage == 1 and not over_dp[i]
            shapes.append(pltpu.VMEM((16, 128) if unused else (*lead, tall, wide), bf16))
        return shapes

    return pl.pallas_call(
        functools.partial(grad_sum_kernel, chunks, n),
        in_specs=[pl.BlockSpec(memory_space=pl.ANY)] * n,
        out_specs=[pl.BlockSpec(memory_space=pltpu.VMEM)] * n,
        out_shape=[jax.ShapeDtypeStruct((r, a.shape[1]), f32) for r, a in zip(rows, arrays)],
        scratch_shapes=[
            *buffers(0),
            *[buffer for stage in range(5) for buffer in buffers(stage)],
            pltpu.SemaphoreType.DMA((len(chunks),)),
            pltpu.SemaphoreType.DMA((5, len(chunks))),
            pltpu.SemaphoreType.DMA((5, len(chunks))),
        ],
        compiler_params=pltpu.CompilerParams(
            collective_id=1, has_side_effects=True, vmem_limit_bytes=56 * MIB
        ),
        cost_estimate=time_of(170),
        name="grad_sums",
    )(*[a.reshape(*d, r, a.shape[1]) for a, d, r in zip(arrays, dims, rows)])


def swap(values):
    return lax.ppermute(values, "dp", [(0, 1), (1, 0)])


def turned(values, dp_count):
    if dp_count != 2:
        return values
    half = values.shape[-1] // 2
    a, b = values[..., :half], values[..., half:]
    first = lax.axis_index("dp") == 0
    return jnp.concatenate([jnp.where(first, a, b), jnp.where(first, b, a)], axis=-1)


def weight_parts(values, axis, dp_count):
    if dp_count != 2:
        return [lax.all_gather(values, "dp", axis=axis, tiled=True)]
    return [values, swap(values)]


def scatter_dp(results, axis):
    if len(results) == 1:
        return lax.psum_scatter(
            results[0]().astype(bf16), "dp", scatter_dimension=axis, tiled=True
        ).astype(f32)
    sent = swap(results[1]().astype(bf16))
    return results[0]() + sent.astype(f32)


def total(terms):
    return functools.reduce(jnp.add, terms)


def heads_apart(values, heads):
    by_head = values.reshape(-1, heads, NOPE + ROPE)
    rows = values.shape[0]
    return jnp.concatenate(
        [by_head[..., :NOPE].reshape(rows, -1), by_head[..., NOPE:].reshape(rows, -1)], axis=1
    )


def heads_together(values, heads):
    rows = values.shape[0]
    nope = values[:, : heads * NOPE].reshape(rows, heads, NOPE)
    rope = values[:, heads * NOPE :].reshape(rows, heads, ROPE)
    return jnp.concatenate([nope, rope], axis=-1).reshape(rows, -1)


def local(
    tokens,
    segments,
    routes,
    combine,
    input_gain,
    query_weight,
    latent_weight,
    latent_gain,
    expand_weight,
    output_weight,
    middle_gain,
    shared_gate,
    shared_up,
    shared_down,
    expert_gate,
    expert_up,
    expert_down,
    cotangent,
):
    _, length, width = tokens.shape
    seq = segments.shape[1]
    top_k = routes.shape[2]
    dp_count = lax.axis_size("dp")
    groups = lax.axis_size("expert")
    shards = dp_count * groups
    both = ("dp", "expert")
    hidden_s = shared_gate.shape[1]
    part_s = hidden_s // groups
    slots = length * top_k * 4 // (groups * 3)
    offset = lax.axis_index("dp") * length
    query_width = query_weight.shape[1]
    heads = query_width // (NOPE + ROPE)
    rows_w = query_weight.shape[0]

    g1 = input_gain.shape[0]
    hits = routes[0][:, None, :] == jnp.arange(groups, dtype=jnp.int32)[None, :, None]
    dense = jnp.sum(jnp.where(hits, combine[0][:, None, :], 0.0), axis=-1)
    dense = jnp.where(jnp.any(hits, axis=-1), dense, -1.0)
    my_weights = lax.all_to_all(dense.T, "expert", split_axis=0, concat_axis=0, tiled=True)
    chosen = my_weights >= 0.0
    before = jnp.arange(length)[:, None] < jnp.arange(length)[None, :]
    place = mm("bt,ts->bs", chosen.astype(bf16), before.astype(bf16)).astype(jnp.int32)
    place = jnp.where(chosen, place, -1)
    place = place[:, None, :]
    row_weights = my_weights[:, None, :]

    linear_width = query_width + RANK + ROPE
    gains = jnp.stack([input_gain, middle_gain, jnp.pad(latent_gain, (0, g1 - latent_gain.size))])
    gains = jnp.pad(gains, ((0, 13), (0, -g1 % 128)))
    own_linear = jnp.concatenate([heads_apart(query_weight, heads), latent_weight], axis=1)
    own_linear = jnp.pad(own_linear, ((0, 0), (0, -linear_width % 128)))
    shares = [gains, own_linear, expand_weight.T]
    if dp_count == 2 and groups == 16:
        shares, down_other = gather_all(shares, expert_down[0])
        down_e = [expert_down[0], down_other]
    else:
        shares = [lax.all_gather(v, both, axis=0, tiled=True) for v in shares]
        down_e = weight_parts(expert_down[0], 1, dp_count)
    gains, query_latent, expand_t = shares
    output_t = lax.all_gather(output_weight.T, both, axis=0, tiled=True)
    gains = gains.reshape(shards, 16, -1)
    first_gain = gains[:, 0, :g1].reshape(-1).astype(f32)
    second_gain = gains[:, 1, :g1].reshape(-1).astype(f32)
    latent_norm = gains[:, 2, : latent_gain.size].reshape(-1).astype(f32)

    shared_own = jnp.stack(
        [
            shared_gate.reshape(rows_w, groups, part_s),
            shared_up.reshape(rows_w, groups, part_s),
            shared_down.T.reshape(rows_w, groups, part_s),
        ],
        axis=1,
    ).transpose(2, 0, 1, 3)
    shared_own = after(shared_own, expand_t)
    shared_cols = shared_moved = lax.all_to_all(shared_own, "expert", split_axis=0, concat_axis=0, tiled=True)
    shared_cols = weight_parts(shared_cols.reshape(groups * rows_w, 3 * part_s), 0, dp_count)
    padded_s = -(-part_s // 128) * 128
    wide_s = [
        jnp.pad(c.reshape(-1, 3, part_s), ((0, 0), (0, 0), (0, padded_s - part_s)))
        for c in shared_cols
    ]
    gate_up_s = [c[:, :2].reshape(-1, 2 * padded_s) for c in wide_s]
    down_s_t = [c[:, 2] for c in wide_s]

    own_e = after((expert_gate[0], expert_up[0]), shared_cols)
    gate_up_e = weight_parts(jnp.concatenate(own_e, axis=1), 0, dp_count)

    token_values = tokens[0].astype(f32)
    scale_one = lax.rsqrt(jnp.mean(token_values * token_values, axis=-1, keepdims=True) + epsilon)
    normed_one = token_values * scale_one
    normed_low = (normed_one * first_gain).astype(bf16)
    own_pos = offset + jnp.arange(length, dtype=jnp.int32)
    cosine, sine = rotary_tables(own_pos)
    tables = (
        jnp.concatenate([cosine] * 4, axis=1),
        jnp.concatenate([-sine, sine, -sine, sine], axis=1),
    )
    linear = mm("rd,dk->rk", normed_low, query_latent)
    latent_raw = linear[:, query_width : query_width + RANK]
    latent_scale = lax.rsqrt(jnp.mean(latent_raw * latent_raw, axis=-1, keepdims=True) + epsilon)
    latent_normed = latent_raw * latent_scale
    latent_low = (latent_normed * latent_norm).astype(bf16)
    rope_low = rotate(linear[:, query_width + RANK : linear_width], cosine, sine).astype(bf16)
    latent_rope = jnp.concatenate([latent_low, rope_low], axis=-1)
    if dp_count == 2:
        other = swap(latent_rope)
        is_first = lax.axis_index("dp") == 0
        latent_rope = jnp.concatenate(
            [jnp.where(is_first, latent_rope, other), jnp.where(is_first, other, latent_rope)]
        )
    else:
        latent_rope = lax.all_gather(latent_rope, "dp", axis=0, tiled=True)
    latent_all = latent_rope[:, :RANK]
    rope_keys = jnp.concatenate([latent_rope[:, RANK:]] * 2, axis=1)
    expanded = mm("rc,kc->rk", latent_all, expand_t).astype(bf16)
    blocks, block_rows, _, _, reach = attention_sizes(length, seq)
    bias = []
    for block in range(blocks):
        start = window_start(block, block_rows, length, seq, reach)
        q_pos = offset + block * block_rows + jnp.arange(block_rows)
        q_seg = lax.dynamic_slice_in_dim(segments[0], offset + block * block_rows, block_rows)
        k_seg = lax.dynamic_slice_in_dim(segments[0], start, reach)
        seen = (q_seg[:, None] == k_seg[None, :]) & (
            q_pos[:, None] >= (start + jnp.arange(reach))[None, :]
        )
        bias.append(jnp.where(seen, 0.0, -1e30).astype(f32))
    bias = jnp.stack(bias)
    mixed = attend(linear, tables, expanded, rope_keys, bias, heads)
    middle = token_values + mm("rv,dv->rd", mixed, output_t)
    scale_two = lax.rsqrt(jnp.mean(middle * middle, axis=-1, keepdims=True) + epsilon)
    normed_two = middle * scale_two
    ffn_rows = (normed_two * second_gain).astype(bf16)

    def gather_rows(values):
        return lax.all_gather(values, "expert", axis=0, tiled=False)

    grads_all = gather_rows(turned(cotangent[0], dp_count))
    rows_all = gather_rows(
        after(turned(ffn_rows, dp_count), (grads_all, shared_moved, my_weights))
    )

    def flat(values):
        return values.reshape(-1, values.shape[-1])

    def scatter_rows(values):
        return lax.psum_scatter(flat(values), "expert", scatter_dimension=0, tiled=True)

    n = len(gate_up_e)
    hidden = expert_gate.shape[2]
    block_of = lambda rows, columns: jax.ShapeDtypeStruct((groups, rows, columns), bf16)
    wide = block_of(slots, hidden)
    wide_shared = block_of(length, padded_s)
    aside = 3 * width // 16
    unit = 2 * groups * width
    picked_grad, d_act = by_block(
        functools.partial(hidden_kernel, n, slots),
        "experts_hidden",
        [place, row_weights, grads_all],
        down_e,
        [block_of(slots, width), wide],
        unit * slots * (length + hidden),
    )
    picked, act_e, d_gate, d_up, act_s, d_shared = by_block(
        functools.partial(forward_kernel, n, slots),
        "experts_forward",
        [place, rows_all, grads_all, d_act],
        [*gate_up_e, *gate_up_s, *down_s_t],
        [block_of(slots, width), wide, wide, wide, wide_shared, block_of(length, 2 * padded_s)],
        unit * (slots * (length + 2 * hidden) + 3 * length * padded_s),
    )
    d_rows = []
    for weights, weights_s in zip(gate_up_e, gate_up_s):
        [part] = by_block(
            functools.partial(rows_kernel, slots),
            "experts_rows",
            [place, d_gate, d_up, d_shared if not d_rows else after(d_shared, part)],
            [weights, weights_s],
            [block_of(length, width // n)],
            unit // n * (slots * (length + 2 * hidden) + 2 * length * padded_s),
        )
        d_rows.append(scatter_rows(part))
    out_parts = by_block(
        functools.partial(output_kernel, n, slots),
        "experts_output",
        [place, row_weights, act_e, act_s],
        [*down_e, *down_s_t],
        [block_of(length, width - aside), block_of(length, aside)],
        unit * (slots * (length + hidden) + length * padded_s),
    )

    column_parts = lambda values: jnp.split(flat(values), n, axis=1)
    picked, picked_grad, rows_parts, grads_parts = map(
        column_parts, (picked, picked_grad, rows_all, grads_all)
    )
    act_e, act_s, d_gate, d_up, d_shared = map(flat, (act_e, act_s, d_gate, d_up, d_shared))
    grad_gate_e = scatter_dp([lambda p=p: mm("rd,rf->df", p, d_gate) for p in picked], 0)
    grad_up_e = scatter_dp([lambda p=p: mm("rd,rf->df", p, d_up) for p in picked], 0)
    grad_down_e = scatter_dp([lambda p=p: mm("rf,rd->fd", act_e, p) for p in picked_grad], 1)
    grad_s = scatter_dp(
        [
            lambda r=r, g=g: jnp.concatenate(
                [mm("rd,rf->df", r, d_shared), mm("rd,rf->df", g, act_s)], axis=1
            )
            for r, g in zip(rows_parts, grads_parts)
        ],
        0,
    )
    grad_s = grad_s.reshape(groups, rows_w, 3, padded_s)[..., :part_s].astype(bf16)
    d_rows[0] = d_rows[0].astype(f32)
    d_rows, grad_gate_e, grad_up_e, grad_down_e, grad_s, out_parts = lax.optimization_barrier(
        (d_rows, grad_gate_e, grad_up_e, grad_down_e, grad_s, out_parts)
    )
    grad_s = lax.all_to_all(grad_s, "expert", split_axis=0, concat_axis=0, tiled=True)
    grad_s = grad_s.transpose(2, 1, 0, 3).reshape(3, rows_w, hidden_s).astype(f32)
    d_rows_own = turned(jnp.concatenate([d.astype(f32) for d in d_rows], axis=1), dp_count)

    out_grad = cotangent[0].astype(f32)
    middle_part, second_gain_grad = norm_back(d_rows_own, normed_two, scale_two, second_gain)
    middle_grad = out_grad + middle_part
    attn_grad = middle_grad.astype(bf16)
    mixed_grad = mm("rd,dv->rv", attn_grad, output_t).astype(bf16)
    attn_parts = jnp.split(turned(attn_grad, dp_count), n, axis=1)
    early = mixed.shape[1] // 2
    grad_out_t = [lambda p=p: mm("rd,rv->dv", p, mixed[:, :early]) for p in attn_parts]
    if dp_count == 2:
        sent, mixed_grad = lax.optimization_barrier((grad_out_t[1]().astype(bf16), mixed_grad))
        grad_out_t = grad_out_t[0]() + swap(sent).astype(f32)
    else:
        grad_out_t = scatter_dp(grad_out_t, 0)
    grad_out_t = [grad_out_t.astype(bf16), mm("rd,rv->dv", attn_grad, mixed[:, early:]).astype(bf16)]
    out_sum = scatter_rows(after(out_parts[0], d_rows))
    d_nope, d_rope, d_expanded, d_keys_rope = attend_back(
        linear, tables, expanded, rope_keys, bias, mixed_grad, heads
    )
    d_expanded, grad_out_t[0] = lax.optimization_barrier((d_expanded, grad_out_t[0]))
    latent_part = mm("rk,kc->rc", d_expanded, expand_t)
    rope_part = d_keys_rope[:, :ROPE] + d_keys_rope[:, ROPE:]
    latent_rope_part = jnp.concatenate([latent_part, rope_part], axis=-1)
    if dp_count == 2:
        first_half, second_half = latent_rope_part[:length], latent_rope_part[length:]
        is_first = lax.axis_index("dp") == 0
        sent = swap(jnp.where(is_first, second_half, first_half).astype(bf16))
        combined = jnp.where(is_first, first_half, second_half) + sent.astype(f32)
    else:
        combined = lax.psum_scatter(latent_rope_part, "dp", scatter_dimension=0, tiled=True)
    grad_expand_t = mm("rk,rc->kc", d_expanded, latent_all).astype(bf16)
    latent_grad, latent_gain_grad = norm_back(
        combined[:, :RANK], latent_normed, latent_scale, latent_norm
    )
    rope_grad = rotate_back(combined[:, RANK:], cosine, sine)
    linear_grad = jnp.concatenate(
        [d_nope, d_rope, latent_grad.astype(bf16), rope_grad.astype(bf16)], axis=-1
    )
    linear_grad = jnp.pad(linear_grad, ((0, 0), (0, -linear_width % 128)))
    normed_grad = mm("rk,dk->rd", linear_grad, query_latent)
    input_part, first_gain_grad = norm_back(normed_grad, normed_one, scale_one, first_gain)
    tokens_grad = (middle_grad + input_part)[None]
    small = jnp.stack(
        [
            first_gain_grad,
            second_gain_grad,
            jnp.pad(
                latent_gain_grad.reshape(shards, -1), ((0, 0), (0, g1 - RANK // shards))
            ).reshape(-1),
        ],
        axis=1,
    )
    small = jnp.pad(small, ((0, 0), (0, -small.shape[1] % 128))).astype(bf16)
    grad_linear = mm("rd,rk->dk", normed_low, linear_grad).astype(bf16)
    sums = [*grad_out_t, flat(out_parts[1]), grad_expand_t, grad_linear, small]
    over_dp = [False, True, False, True, True, True]
    if dp_count == 2 and groups == 16:
        sums = grad_sums(sums, over_dp)
    else:
        sums = [
            lax.psum_scatter(v, both if o else "expert", scatter_dimension=0, tiled=True)
            for v, o in zip(sums, over_dp)
        ]
        sums = [v.astype(f32) for v in sums]
    *grad_out_t, out_aside, grad_expand_t, grad_linear, small = sums
    out_sum = after(out_sum, grad_linear)
    out_sum = jnp.concatenate([out_sum.astype(f32), out_aside], axis=1)
    outputs = (middle + turned(out_sum, dp_count)).astype(bf16)[None]
    return (
        outputs,
        tokens_grad,
        small[:, 0],
        heads_together(grad_linear[:, :query_width], heads),
        grad_linear[:, query_width:linear_width],
        small[: RANK // shards, 2],
        grad_expand_t.T,
        jnp.concatenate(grad_out_t, axis=1).T,
        small[:, 1],
        grad_s[0],
        grad_s[1],
        grad_s[2].T,
        grad_gate_e[None],
        grad_up_e[None],
        grad_down_e[None],
    )


def solution(mesh):
    rows = P("expert", "dp", None)
    first = P(("dp", "expert"), None)
    last = P(None, ("dp", "expert"))
    vector = P(("dp", "expert"))
    down = P("expert", None, "dp")
    return jax.shard_map(
        local,
        mesh=mesh,
        in_specs=(
            rows,
            P("expert", None),
            rows,
            rows,
            vector,
            first,
            first,
            vector,
            last,
            last,
            vector,
            first,
            first,
            last,
            rows,
            rows,
            down,
            rows,
        ),
        out_specs=(
            rows,
            rows,
            vector,
            first,
            first,
            vector,
            last,
            last,
            vector,
            first,
            first,
            last,
            rows,
            rows,
            down,
        ),
        check_vma=False,
    )
```

```python
import functools

import jax
import jax.numpy as jnp
from jax import lax
from jax.experimental import pallas as pl
from jax.experimental.pallas import tpu as pltpu
from jax.sharding import PartitionSpec as P

NOPE = 128
ROPE = 64
VDIM = 128
RANK = 512
DOC = 512
epsilon = 1e-06
f32 = jnp.float32
bf16 = jnp.bfloat16
MIB = 1 << 20
TILE = 256


def mm(spec, a, b):
    return jnp.einsum(spec, a, b, preferred_element_type=f32)


def dot(a, b, ca, cb):
    return lax.dot_general(a, b, (((ca,), (cb,)), ((), ())), preferred_element_type=f32)


def after(values, earlier):
    return lax.optimization_barrier((values, earlier))[0]


def rotate(values, cosine, sine):
    half = values.shape[-1] // 2
    a, b = values[..., :half], values[..., half:]
    return jnp.concatenate([a * cosine - b * sine, b * cosine + a * sine], axis=-1)


def rotate_back(values, cosine, sine):
    return rotate(values, cosine, -sine)


def norm_back(gradient, normed, scale_vec, gain_vec):
    scaled = gradient * gain_vec
    inner = jnp.mean(scaled * normed, axis=-1, keepdims=True)
    return scale_vec * (scaled - normed * inner), jnp.sum(gradient * normed, axis=0)


def silu_parts(gate_in):
    sig = jax.nn.sigmoid(gate_in)
    return gate_in * sig, sig * (1.0 + gate_in * (1.0 - sig))


def rotary_tables(positions):
    frequency = jnp.power(10000.0, -jnp.arange(ROPE // 2).astype(f32) * 2.0 / ROPE)
    angles = positions.astype(f32)[:, None] * frequency[None, :]
    return jnp.cos(angles), jnp.sin(angles)


def window_start(block, rows, length, seq, reach):
    first = lax.axis_index("dp") * length + block * rows - DOC
    return jnp.clip(first, 0, seq - reach)


def swap_halves(values):
    lane = lax.broadcasted_iota(jnp.int32, values.shape, 1)
    up = pltpu.roll(values, ROPE // 2, 1)
    down = pltpu.roll(values, 2 * ROPE - ROPE // 2, 1)
    return jnp.where(lane % ROPE < ROPE // 2, down, up)


def head_lanes(shape, head):
    lane = lax.broadcasted_iota(jnp.int32, shape, 1)
    return (lane // ROPE) == head


def probabilities(q, qr, k, kr, bias):
    scores = (dot(q, k, 1, 1) + dot(qr, kr, 1, 1)) * (NOPE + ROPE) ** (-0.5) + bias
    exponent = jnp.exp(scores - jnp.max(scores, axis=-1, keepdims=True))
    return exponent / jnp.sum(exponent, axis=-1, keepdims=True)


def attend_kernel(sizes, nope_ref, rope_ref, cos_ref, sin_ref, kv_ref, kr_ref, bias_ref, out_ref):
    blocks, rows, length, seq, reach = sizes
    for block in range(blocks):
        at = pl.ds(block * rows, rows)
        rope = rope_ref[at, :]
        rope = (rope * cos_ref[at, :] + swap_halves(rope) * sin_ref[at, :]).astype(bf16)
        start = pl.multiple_of(window_start(block, rows, length, seq, reach), 128)
        span = pl.ds(start, reach)
        kr = kr_ref[span, :]
        for head in range(2):
            qr = jnp.where(head_lanes(rope.shape, head), rope, jnp.zeros_like(rope))
            q = nope_ref[at, head * NOPE : (head + 1) * NOPE].astype(bf16)
            k = kv_ref[span, head * 256 : head * 256 + NOPE]
            v = kv_ref[span, head * 256 + NOPE : (head + 1) * 256]
            probs = probabilities(q, qr, k, kr, bias_ref[block])
            out_ref[at, head * VDIM : (head + 1) * VDIM] = dot(
                probs.astype(bf16), v, 1, 0
            ).astype(bf16)


def attend_back_kernel(
    sizes,
    nope_ref,
    rope_ref,
    cos_ref,
    sin_ref,
    kv_ref,
    kr_ref,
    bias_ref,
    grad_ref,
    dnope_ref,
    drope_ref,
    dkv_ref,
    dkr_ref,
    dk_acc,
    dv_acc,
):
    blocks, rows, length, seq, reach = sizes
    factor = (NOPE + ROPE) ** (-0.5)

    @pl.when(pl.program_id(0) == 0)
    def _():
        dkr_ref[...] = jnp.zeros_like(dkr_ref)

    dk_acc[...] = jnp.zeros_like(dk_acc)
    dv_acc[...] = jnp.zeros_like(dv_acc)
    for block in range(blocks):
        at = pl.ds(block * rows, rows)
        rope = rope_ref[at, :]
        rope = (rope * cos_ref[at, :] + swap_halves(rope) * sin_ref[at, :]).astype(bf16)
        start = pl.multiple_of(window_start(block, rows, length, seq, reach), 128)
        span = pl.ds(start, reach)
        kr = kr_ref[span, :]
        rope_grad = jnp.zeros((rows, 2 * ROPE), f32)
        for head in range(2):
            mine = head_lanes(rope.shape, head)
            qr = jnp.where(mine, rope, jnp.zeros_like(rope))
            q = nope_ref[at, head * NOPE : (head + 1) * NOPE].astype(bf16)
            k = kv_ref[span, head * 256 : head * 256 + NOPE]
            v = kv_ref[span, head * 256 + NOPE : (head + 1) * 256]
            grad = grad_ref[at, head * VDIM : (head + 1) * VDIM]
            probs = probabilities(q, qr, k, kr, bias_ref[block])
            dprobs = dot(grad, v, 1, 1)
            inner = jnp.sum(dprobs * probs, axis=-1, keepdims=True)
            dscores = (probs * (dprobs - inner) * factor).astype(bf16)
            dnope_ref[at, head * NOPE : (head + 1) * NOPE] = dot(dscores, k, 1, 0).astype(bf16)
            rope_grad += jnp.where(mine, dot(dscores, kr, 1, 0), 0.0)
            dk_acc[head, span, :] += dot(dscores, q, 0, 0)
            dv_acc[head, span, :] += dot(probs.astype(bf16), grad, 0, 0)
            dkr_ref[span, :] += dot(dscores, qr, 0, 0)
        rope_grad = rope_grad * cos_ref[at, :] - swap_halves(rope_grad) * sin_ref[at, :]
        drope_ref[at, :] = rope_grad.astype(bf16)
    for head in range(2):
        dkv_ref[:, head * 256 : head * 256 + NOPE] = dk_acc[head].astype(bf16)
        dkv_ref[:, head * 256 + NOPE : (head + 1) * 256] = dv_acc[head].astype(bf16)


def attention_sizes(length, seq):
    rows = min(256, length)
    return length // rows, rows, length, seq, min(seq, rows + DOC)


def attention_specs(length, seq, heads, sizes):
    first_rope = heads * NOPE // (2 * ROPE)
    whole = lambda shape: pl.BlockSpec(shape, lambda p: (0,) * len(shape))
    return [
        pl.BlockSpec((length, 2 * NOPE), lambda p: (0, p)),
        pl.BlockSpec((length, 2 * ROPE), lambda p: (0, first_rope + p)),
        whole((length, 2 * ROPE)),
        whole((length, 2 * ROPE)),
        pl.BlockSpec((seq, 2 * (NOPE + VDIM)), lambda p: (0, p)),
        whole((seq, 2 * ROPE)),
        whole((sizes[0], sizes[1], sizes[4])),
    ]


def attend(linear, tables, kv, kr, bias, heads):
    length, seq = linear.shape[0], kv.shape[0]
    sizes = attention_sizes(length, seq)
    return pl.pallas_call(
        functools.partial(attend_kernel, sizes),
        grid=(heads // 2,),
        in_specs=attention_specs(length, seq, heads, sizes),
        out_specs=pl.BlockSpec((length, 2 * VDIM), lambda p: (0, p)),
        out_shape=jax.ShapeDtypeStruct((length, heads * VDIM), bf16),
        compiler_params=pltpu.CompilerParams(vmem_limit_bytes=48 * MIB),
        cost_estimate=time_of(27),
        name="attend",
    )(linear, linear, *tables, kv, kr, bias)


def attend_back(linear, tables, kv, kr, bias, grad, heads):
    length, seq = linear.shape[0], kv.shape[0]
    sizes = attention_sizes(length, seq)
    return pl.pallas_call(
        functools.partial(attend_back_kernel, sizes),
        grid=(heads // 2,),
        in_specs=attention_specs(length, seq, heads, sizes)
        + [pl.BlockSpec((length, 2 * VDIM), lambda p: (0, p))],
        out_specs=[
            pl.BlockSpec((length, 2 * NOPE), lambda p: (0, p)),
            pl.BlockSpec((length, 2 * ROPE), lambda p: (0, p)),
            pl.BlockSpec((seq, 2 * (NOPE + VDIM)), lambda p: (0, p)),
            pl.BlockSpec((seq, 2 * ROPE), lambda p: (0, 0)),
        ],
        out_shape=[
            jax.ShapeDtypeStruct((length, heads * NOPE), bf16),
            jax.ShapeDtypeStruct((length, heads * ROPE), bf16),
            jax.ShapeDtypeStruct((seq, heads * (NOPE + VDIM)), bf16),
            jax.ShapeDtypeStruct((seq, 2 * ROPE), f32),
        ],
        scratch_shapes=[pltpu.VMEM((2, seq, NOPE), f32), pltpu.VMEM((2, seq, VDIM), f32)],
        compiler_params=pltpu.CompilerParams(vmem_limit_bytes=48 * MIB),
        cost_estimate=time_of(51),
        name="attend_back",
    )(linear, linear, *tables, kv, kr, bias, grad)


def one_hot(place_ref, slots):
    place = place_ref[0]
    slot = lax.broadcasted_iota(jnp.int32, (slots, place.shape[1]), 0)
    return slot == place


def width_parts(refs, width):
    step = width // len(refs)
    return [(ref, pl.ds(i * step, step)) for i, ref in enumerate(refs)]


def hidden_kernel(n, slots, place_ref, weight_ref, grads_ref, *refs):
    down, (picked_ref, d_act_ref) = refs[:n], refs[n:]
    width = grads_ref.shape[-1]
    hot = one_hot(place_ref, slots)
    slot_weight = jnp.sum(jnp.where(hot, weight_ref[0], 0.0), axis=1, keepdims=True)
    picks = hot.astype(f32).astype(bf16)
    picked_ref[0] = (dot(picks, grads_ref[0], 1, 0) * slot_weight).astype(bf16)
    d_act = total([dot(picked_ref[0, :, at], w[...], 1, 1) for w, at in width_parts(down, width)])
    d_act_ref[0] = d_act.astype(bf16)


def gated_tiles(values_ref, weights, d_act, act_ref, d_gate_ref, d_up_ref, up_first):
    width, hidden = values_ref.shape[-1], act_ref.shape[-1]
    for left in range(0, hidden, TILE):
        wide = min(TILE, hidden - left)
        here, above = pl.ds(left, wide), pl.ds(hidden + left, wide)
        parts = width_parts(weights, width)
        gate = total([dot(values_ref[0, :, at], w[:, here], 1, 0) for w, at in parts])
        up = total([dot(values_ref[0, :, at], w[:, above], 1, 0) for w, at in parts])
        silu, slope = silu_parts(gate)
        d_tile = d_act[:, left : left + wide].astype(f32)
        act_ref[0, :, here] = (silu * up).astype(bf16)
        d_gate_ref[0, :, here] = (d_tile * up * slope).astype(bf16)
        d_up_ref[0, :, pl.ds(up_first + left, wide)] = (d_tile * silu).astype(bf16)


def forward_kernel(n, slots, place_ref, rows_ref, grads_ref, d_act_ref, *refs):
    weights, shared, down_s, outs = refs[:n], refs[n : 2 * n], refs[2 * n : 3 * n], refs[3 * n :]
    picked_ref, act_ref, d_gate_ref, d_up_ref, act_s_ref, d_shared_ref = outs
    picks = one_hot(place_ref, slots).astype(f32).astype(bf16)
    picked_ref[0] = dot(picks, rows_ref[0], 1, 0).astype(bf16)
    gated_tiles(picked_ref, weights, d_act_ref.at[0], act_ref, d_gate_ref, d_up_ref, 0)
    half = act_s_ref.shape[-1]
    parts = width_parts(down_s, rows_ref.shape[-1])
    d_act_s = total([dot(grads_ref[0, :, at], w[...], 1, 0) for w, at in parts])
    gated_tiles(rows_ref, shared, d_act_s, act_s_ref, d_shared_ref, d_shared_ref, half)


def rows_kernel(
    slots, place_ref, d_gate_ref, d_up_ref, d_shared_ref, gate_up_ref, gate_up_s_ref, d_rows_ref
):
    picks = one_hot(place_ref, slots).astype(f32).astype(bf16)
    d_both = jnp.concatenate([d_gate_ref[0], d_up_ref[0]], axis=1)
    d_row = dot(d_both, gate_up_ref[...], 1, 1).astype(bf16)
    d_rows_ref[0] = (
        dot(picks, d_row, 0, 0) + dot(d_shared_ref[0], gate_up_s_ref[...], 1, 1)
    ).astype(bf16)


def output_kernel(n, slots, place_ref, weight_ref, act_ref, act_s_ref, *refs):
    down, down_s, outs = refs[:n], refs[n : 2 * n], refs[2 * n :]
    hot = one_hot(place_ref, slots)
    slot_weight = jnp.sum(jnp.where(hot, weight_ref[0], 0.0), axis=1, keepdims=True)
    picks = hot.astype(f32).astype(bf16)
    bounds = [0, outs[0].shape[-1], outs[0].shape[-1] + outs[1].shape[-1]]
    for i, (w, w_s) in enumerate(zip(down, down_s)):
        out = (dot(act_ref[0], w[...], 1, 0) * slot_weight).astype(bf16)
        rows = (dot(picks, out, 0, 0) + dot(act_s_ref[0], w_s[...], 1, 1)).astype(bf16)
        first = i * w.shape[1]
        for out_ref, low, high in zip(outs, bounds, bounds[1:]):
            low_in, high_in = max(low, first), min(high, first + w.shape[1])
            if low_in < high_in:
                out_ref[0, :, low_in - low : high_in - low] = rows[:, low_in - first : high_in - first]


def by_block(kernel, name, blocked, fixed, outs, flops):
    count = blocked[0].shape[0]
    block = lambda a: pl.BlockSpec((1, *a.shape[1:]), lambda b: (b, 0, 0))
    stay = lambda a: pl.BlockSpec(a.shape, lambda b: (0, 0), pipeline_mode=pl.Buffered(1))
    moved = sum(a.size * a.dtype.itemsize for a in (*blocked, *fixed, *outs))
    return pl.pallas_call(
        kernel,
        grid=(count,),
        in_specs=[block(a) for a in blocked] + [stay(a) for a in fixed],
        out_specs=[block(a) for a in outs],
        out_shape=outs,
        compiler_params=pltpu.CompilerParams(vmem_limit_bytes=60 * MIB),
        cost_estimate=pl.CostEstimate(flops=flops, bytes_accessed=moved, transcendentals=0),
        name=name,
    )(*blocked, *fixed)


def neighbours():
    dp, expert = lax.axis_index("dp"), lax.axis_index("expert")
    core, y = expert % 2, (expert // 2) % 2
    z_low, z_high = (expert // 4) % 2, expert // 8
    partners = [
        {"expert": expert + 1 - 2 * core},
        {"dp": 1 - dp},
        {"expert": expert + 2 - 4 * y},
        {"expert": expert + 4 - 8 * z_low},
        {"expert": expert + 8 - 16 * z_high},
    ]
    barrier = pltpu.get_barrier_semaphore()
    for partner in partners:
        pl.semaphore_signal(barrier, inc=1, device_id=partner, device_id_type=pl.DeviceIdType.MESH)
    pl.semaphore_wait(barrier, len(partners))
    return partners, (core, dp, y, z_low, z_high)


PIECE = 64 * 1024


def chunks_of(shapes):
    chunks = []
    for i, (rows, columns) in enumerate(shapes):
        wide = min(columns, 1024)
        tall = rows
        while tall > 16 and tall * wide > PIECE:
            tall //= 2
        chunks += [
            (i, top, tall, left, min(wide, columns - left))
            for top in range(0, rows, tall)
            for left in range(0, columns, wide)
        ]
    return chunks


def piece_of(chunk):
    _, top, tall, left, wide = chunk
    return pl.ds(top, tall), pl.ds(left, wide)


def time_of(microseconds):
    return pl.CostEstimate(
        flops=0, bytes_accessed=int(microseconds * 3.69e6), transcendentals=0
    )


def gather_kernel(chunks, n, *refs):
    ins, outs = refs[:n], refs[n + 1 : 2 * n + 1]
    own_sem, send_sem, recv_sem, cross_sem = refs[2 * n + 2 :]
    partners, (core, dp, y, z_low, z_high) = neighbours()
    crossing = pltpu.make_async_remote_copy(
        src_ref=refs[n],
        dst_ref=refs[2 * n + 1],
        send_sem=cross_sem.at[0],
        recv_sem=cross_sem.at[1],
        device_id=partners[1],
        device_id_type=pl.DeviceIdType.MESH,
    )
    crossing.start()
    mine = (dp, z_high, z_low, y, core)
    place = [4, 0, 3, 2, 1]
    own = [pltpu.make_async_copy(ins[i], outs[i].at[mine], own_sem.at[i]) for i in range(n)]
    for copy in own:
        copy.start()
    copies = {}
    waited = set()
    count = len(chunks)

    def order(k):
        return [4, 2, 3, 1, 0] if k % 2 else [4, 3, 2, 1, 0]

    for turn in range(count + 5):
        for stage in range(5):
            k = turn - stage
            if not 0 <= k < count:
                continue
            array = chunks[k][0]
            gathered = [place[axis] for axis in order(k)[:stage]]
            held = [slice(None) if d in gathered else mine[d] for d in range(5)]
            there = outs[array].at[(*held, *piece_of(chunks[k]))]
            if stage == 0:
                here = ins[array].at[piece_of(chunks[k])]
            else:
                here = there
                copies[stage - 1, k].wait_recv()
            if stage == 1 and array not in waited:
                waited.add(array)
                own[array].wait()
            copies[stage, k] = pltpu.make_async_remote_copy(
                src_ref=here,
                dst_ref=there,
                send_sem=send_sem.at[stage, k],
                recv_sem=recv_sem.at[stage, k],
                device_id=partners[order(k)[stage]],
                device_id_type=pl.DeviceIdType.MESH,
            )
            copies[stage, k].start()
    for k in range(count):
        copies[4, k].wait_recv()
    for copy in copies.values():
        copy.wait_send()
    crossing.wait()


def gather_all(arrays, crossed):
    chunks = chunks_of([a.shape for a in arrays])
    dims = (2, 2, 2, 2, 2)
    n = len(arrays)
    *gathered, crossed = pl.pallas_call(
        functools.partial(gather_kernel, chunks, n),
        in_specs=[pl.BlockSpec(memory_space=pl.ANY)] * (n + 1),
        out_specs=[pl.BlockSpec(memory_space=pl.ANY)] * (n + 1),
        out_shape=[
            *[jax.ShapeDtypeStruct((*dims, *a.shape), a.dtype) for a in arrays],
            jax.ShapeDtypeStruct(crossed.shape, crossed.dtype),
        ],
        scratch_shapes=[
            pltpu.SemaphoreType.DMA((n,)),
            pltpu.SemaphoreType.DMA((5, len(chunks))),
            pltpu.SemaphoreType.DMA((5, len(chunks))),
            pltpu.SemaphoreType.DMA((2,)),
        ],
        compiler_params=pltpu.CompilerParams(collective_id=2, has_side_effects=True),
        cost_estimate=time_of(180),
        name="gather_all",
    )(*arrays, crossed)
    return [g.reshape(-1, a.shape[1]) for g, a in zip(gathered, arrays)], crossed


def add_rows(into, left, right):
    step = 16
    lead = (slice(None),) * (len(into.shape) - 2)

    @pl.loop(0, into.shape[-2] // step)
    def _(i):
        at = (*lead, pl.ds(pl.multiple_of(i * step, step), step), slice(None))
        into[at] = (left[at].astype(f32) + right[at].astype(f32)).astype(into.dtype)


def grad_sum_kernel(chunks, n, *refs):
    ins, outs = refs[:n], refs[n : 2 * n]
    count = len(chunks)
    own = refs[2 * n : 2 * n + count]
    got = [refs[2 * n + (i + 1) * count :][:count] for i in range(5)]
    load_sem, send_sem, recv_sem = refs[-3:]
    partners, mine = neighbours()
    core = mine[0]

    def source(k, which):
        array = chunks[k][0]
        lead = (slice(None),) * (len(ins[array].shape) - 3)
        return ins[array].at[(*lead, which, *piece_of(chunks[k]))]

    def pick(ref, stage, which):
        lead = [0, 0, 2, 1, 0][stage]
        return ref.at[(*(slice(None),) * lead, which)]

    def stages(k):
        return [0, 1, 2, 3, 4] if len(ins[chunks[k][0]].shape) == 7 else [0, 2, 3, 4]

    copies = {}

    def start(stage, k, values):
        copies[stage, k] = pltpu.make_async_remote_copy(
            src_ref=values,
            dst_ref=got[stage][k],
            send_sem=send_sem.at[stage, k],
            recv_sem=recv_sem.at[stage, k],
            device_id=partners[stage],
            device_id_type=pl.DeviceIdType.MESH,
        )
        copies[stage, k].start()

    loads = [pltpu.make_async_copy(source(k, core), own[k], load_sem.at[k]) for k in range(count)]
    for k in range(count):
        start(0, k, source(k, 1 - core))
        loads[k].start()
    for turn in range(count + 4):
        for step in range(5):
            k = turn - step
            if not 0 <= k < count or step >= len(stages(k)):
                continue
            stage = stages(k)[step]
            later = stages(k)[step + 1] if step + 1 < len(stages(k)) else None
            held = got[stage][k]
            copies[stage, k].wait_recv()
            if step == 0:
                loads[k].wait()
                sent, kept = 1 - mine[later], mine[later]
                part = pick(held, later, sent)
                add_rows(part, part, pick(own[k], later, sent))
                start(later, k, part)
                part = pick(held, later, kept)
                add_rows(part, part, pick(own[k], later, kept))
                continue
            kept = pick(got[stages(k)[step - 1]][k], stage, mine[stage])
            if later is None:
                add_rows(outs[chunks[k][0]].at[piece_of(chunks[k])], held, kept)
            else:
                add_rows(held, held, kept)
                start(later, k, pick(held, later, 1 - mine[later]))
    for copy in copies.values():
        copy.wait_send()


def grad_sums(arrays, over_dp):
    n = len(arrays)
    dims = [(2,) * (5 if o else 4) for o in over_dp]
    rows = [a.shape[0] // 2 ** len(d) for a, d in zip(arrays, dims)]
    chunks = chunks_of([(r, a.shape[1]) for r, a in zip(rows, arrays)])
    wider = [c for c in chunks if over_dp[c[0]]]
    narrower = [c for c in chunks if not over_dp[c[0]]]
    chunks = []
    while wider or narrower:
        chunks += wider[:1] + narrower[:1]
        wider, narrower = wider[1:], narrower[1:]

    def buffers(stage):
        shapes = []
        for i, _, tall, _, wide in chunks:
            lead = dims[i][:-1] if stage == 0 else (2,) * (4 - stage)
            unused = stage == 1 and not over_dp[i]
            shapes.append(pltpu.VMEM((16, 128) if unused else (*lead, tall, wide), bf16))
        return shapes

    return pl.pallas_call(
        functools.partial(grad_sum_kernel, chunks, n),
        in_specs=[pl.BlockSpec(memory_space=pl.ANY)] * n,
        out_specs=[pl.BlockSpec(memory_space=pltpu.VMEM)] * n,
        out_shape=[jax.ShapeDtypeStruct((r, a.shape[1]), f32) for r, a in zip(rows, arrays)],
        scratch_shapes=[
            *buffers(0),
            *[buffer for stage in range(5) for buffer in buffers(stage)],
            pltpu.SemaphoreType.DMA((len(chunks),)),
            pltpu.SemaphoreType.DMA((5, len(chunks))),
            pltpu.SemaphoreType.DMA((5, len(chunks))),
        ],
        compiler_params=pltpu.CompilerParams(
            collective_id=1, has_side_effects=True, vmem_limit_bytes=56 * MIB
        ),
        cost_estimate=time_of(170),
        name="grad_sums",
    )(*[a.reshape(*d, r, a.shape[1]) for a, d, r in zip(arrays, dims, rows)])


def swap(values):
    return lax.ppermute(values, "dp", [(0, 1), (1, 0)])


def turned(values, dp_count):
    if dp_count != 2:
        return values
    half = values.shape[-1] // 2
    a, b = values[..., :half], values[..., half:]
    first = lax.axis_index("dp") == 0
    return jnp.concatenate([jnp.where(first, a, b), jnp.where(first, b, a)], axis=-1)


def weight_parts(values, axis, dp_count):
    if dp_count != 2:
        return [lax.all_gather(values, "dp", axis=axis, tiled=True)]
    return [values, swap(values)]


def scatter_dp(results, axis):
    if len(results) == 1:
        return lax.psum_scatter(
            results[0]().astype(bf16), "dp", scatter_dimension=axis, tiled=True
        ).astype(f32)
    sent = swap(results[1]().astype(bf16))
    return results[0]() + sent.astype(f32)


def total(terms):
    return functools.reduce(jnp.add, terms)


def heads_apart(values, heads):
    by_head = values.reshape(-1, heads, NOPE + ROPE)
    rows = values.shape[0]
    return jnp.concatenate(
        [by_head[..., :NOPE].reshape(rows, -1), by_head[..., NOPE:].reshape(rows, -1)], axis=1
    )


def heads_together(values, heads):
    rows = values.shape[0]
    nope = values[:, : heads * NOPE].reshape(rows, heads, NOPE)
    rope = values[:, heads * NOPE :].reshape(rows, heads, ROPE)
    return jnp.concatenate([nope, rope], axis=-1).reshape(rows, -1)


def local(
    tokens,
    segments,
    routes,
    combine,
    input_gain,
    query_weight,
    latent_weight,
    latent_gain,
    expand_weight,
    output_weight,
    middle_gain,
    shared_gate,
    shared_up,
    shared_down,
    expert_gate,
    expert_up,
    expert_down,
    cotangent,
):
    _, length, width = tokens.shape
    seq = segments.shape[1]
    top_k = routes.shape[2]
    dp_count = lax.axis_size("dp")
    groups = lax.axis_size("expert")
    shards = dp_count * groups
    both = ("dp", "expert")
    hidden_s = shared_gate.shape[1]
    part_s = hidden_s // groups
    slots = length * top_k * 4 // (groups * 3)
    offset = lax.axis_index("dp") * length
    query_width = query_weight.shape[1]
    heads = query_width // (NOPE + ROPE)
    rows_w = query_weight.shape[0]

    g1 = input_gain.shape[0]
    hits = routes[0][:, None, :] == jnp.arange(groups, dtype=jnp.int32)[None, :, None]
    dense = jnp.sum(jnp.where(hits, combine[0][:, None, :], 0.0), axis=-1)
    dense = jnp.where(jnp.any(hits, axis=-1), dense, -1.0)
    my_weights = lax.all_to_all(dense.T, "expert", split_axis=0, concat_axis=0, tiled=True)
    chosen = my_weights >= 0.0
    before = jnp.arange(length)[:, None] < jnp.arange(length)[None, :]
    place = mm("bt,ts->bs", chosen.astype(bf16), before.astype(bf16)).astype(jnp.int32)
    place = jnp.where(chosen, place, -1)
    place = place[:, None, :]
    row_weights = my_weights[:, None, :]

    linear_width = query_width + RANK + ROPE
    gains = jnp.stack([input_gain, middle_gain, jnp.pad(latent_gain, (0, g1 - latent_gain.size))])
    gains = jnp.pad(gains, ((0, 13), (0, -g1 % 128)))
    own_linear = jnp.concatenate([heads_apart(query_weight, heads), latent_weight], axis=1)
    own_linear = jnp.pad(own_linear, ((0, 0), (0, -linear_width % 128)))
    shares = [gains, own_linear, expand_weight.T]
    if dp_count == 2 and groups == 16:
        shares, down_other = gather_all(shares, expert_down[0])
        down_e = [expert_down[0], down_other]
    else:
        shares = [lax.all_gather(v, both, axis=0, tiled=True) for v in shares]
        down_e = weight_parts(expert_down[0], 1, dp_count)
    gains, query_latent, expand_t = shares
    def gather_rows(values):
        return lax.all_gather(values, "expert", axis=0, tiled=False)

    grads_all = gather_rows(turned(cotangent[0], dp_count))
    output_t = after(output_weight, (grads_all, query_latent)).T
    output_t = lax.all_gather(output_t, both, axis=0, tiled=True)
    gains = gains.reshape(shards, 16, -1)
    first_gain = gains[:, 0, :g1].reshape(-1).astype(f32)
    second_gain = gains[:, 1, :g1].reshape(-1).astype(f32)
    latent_norm = gains[:, 2, : latent_gain.size].reshape(-1).astype(f32)

    shared_own = jnp.stack(
        [
            shared_gate.reshape(rows_w, groups, part_s),
            shared_up.reshape(rows_w, groups, part_s),
            shared_down.T.reshape(rows_w, groups, part_s),
        ],
        axis=1,
    ).transpose(2, 0, 1, 3)
    shared_own = after(shared_own, expand_t)
    shared_cols = shared_moved = lax.all_to_all(shared_own, "expert", split_axis=0, concat_axis=0, tiled=True)
    shared_cols = weight_parts(shared_cols.reshape(groups * rows_w, 3 * part_s), 0, dp_count)
    padded_s = -(-part_s // 128) * 128
    wide_s = [
        jnp.pad(c.reshape(-1, 3, part_s), ((0, 0), (0, 0), (0, padded_s - part_s)))
        for c in shared_cols
    ]
    gate_up_s = [c[:, :2].reshape(-1, 2 * padded_s) for c in wide_s]
    down_s_t = [c[:, 2] for c in wide_s]

    own_e = after((expert_gate[0], expert_up[0]), shared_cols)
    gate_up_e = weight_parts(jnp.concatenate(own_e, axis=1), 0, dp_count)

    token_values = tokens[0].astype(f32)
    scale_one = lax.rsqrt(jnp.mean(token_values * token_values, axis=-1, keepdims=True) + epsilon)
    normed_one = token_values * scale_one
    normed_low = (normed_one * first_gain).astype(bf16)
    own_pos = offset + jnp.arange(length, dtype=jnp.int32)
    cosine, sine = rotary_tables(own_pos)
    tables = (
        jnp.concatenate([cosine] * 4, axis=1),
        jnp.concatenate([-sine, sine, -sine, sine], axis=1),
    )
    linear = mm("rd,dk->rk", normed_low, query_latent)
    latent_raw = linear[:, query_width : query_width + RANK]
    latent_scale = lax.rsqrt(jnp.mean(latent_raw * latent_raw, axis=-1, keepdims=True) + epsilon)
    latent_normed = latent_raw * latent_scale
    latent_low = (latent_normed * latent_norm).astype(bf16)
    rope_low = rotate(linear[:, query_width + RANK : linear_width], cosine, sine).astype(bf16)
    latent_rope = jnp.concatenate([latent_low, rope_low], axis=-1)
    if dp_count == 2:
        other = swap(latent_rope)
        is_first = lax.axis_index("dp") == 0
        latent_rope = jnp.concatenate(
            [jnp.where(is_first, latent_rope, other), jnp.where(is_first, other, latent_rope)]
        )
    else:
        latent_rope = lax.all_gather(latent_rope, "dp", axis=0, tiled=True)
    latent_all = latent_rope[:, :RANK]
    rope_keys = jnp.concatenate([latent_rope[:, RANK:]] * 2, axis=1)
    expanded = mm("rc,kc->rk", latent_all, expand_t).astype(bf16)
    blocks, block_rows, _, _, reach = attention_sizes(length, seq)
    bias = []
    for block in range(blocks):
        start = window_start(block, block_rows, length, seq, reach)
        q_pos = offset + block * block_rows + jnp.arange(block_rows)
        q_seg = lax.dynamic_slice_in_dim(segments[0], offset + block * block_rows, block_rows)
        k_seg = lax.dynamic_slice_in_dim(segments[0], start, reach)
        seen = (q_seg[:, None] == k_seg[None, :]) & (
            q_pos[:, None] >= (start + jnp.arange(reach))[None, :]
        )
        bias.append(jnp.where(seen, 0.0, -1e30).astype(f32))
    bias = jnp.stack(bias)
    mixed = attend(linear, tables, expanded, rope_keys, bias, heads)
    middle = token_values + mm("rv,dv->rd", mixed, output_t)
    scale_two = lax.rsqrt(jnp.mean(middle * middle, axis=-1, keepdims=True) + epsilon)
    normed_two = middle * scale_two
    ffn_rows = (normed_two * second_gain).astype(bf16)

    rows_all = gather_rows(
        after(turned(ffn_rows, dp_count), (grads_all, shared_moved, my_weights))
    )

    def flat(values):
        return values.reshape(-1, values.shape[-1])

    def scatter_rows(values):
        return lax.psum_scatter(flat(values), "expert", scatter_dimension=0, tiled=True)

    n = len(gate_up_e)
    hidden = expert_gate.shape[2]
    block_of = lambda rows, columns: jax.ShapeDtypeStruct((groups, rows, columns), bf16)
    wide = block_of(slots, hidden)
    wide_shared = block_of(length, padded_s)
    aside = 3 * width // 16
    unit = 2 * groups * width
    picked_grad, d_act = by_block(
        functools.partial(hidden_kernel, n, slots),
        "experts_hidden",
        [place, row_weights, grads_all],
        down_e,
        [block_of(slots, width), wide],
        unit * slots * (length + hidden),
    )
    picked, act_e, d_gate, d_up, act_s, d_shared = by_block(
        functools.partial(forward_kernel, n, slots),
        "experts_forward",
        [place, rows_all, grads_all, d_act],
        [*gate_up_e, *gate_up_s, *down_s_t],
        [block_of(slots, width), wide, wide, wide, wide_shared, block_of(length, 2 * padded_s)],
        unit * (slots * (length + 2 * hidden) + 3 * length * padded_s),
    )
    d_rows = []
    for weights, weights_s in zip(gate_up_e, gate_up_s):
        [part] = by_block(
            functools.partial(rows_kernel, slots),
            "experts_rows",
            [place, d_gate, d_up, d_shared if not d_rows else after(d_shared, part)],
            [weights, weights_s],
            [block_of(length, width // n)],
            unit // n * (slots * (length + 2 * hidden) + 2 * length * padded_s),
        )
        d_rows.append(scatter_rows(part))
    out_parts = by_block(
        functools.partial(output_kernel, n, slots),
        "experts_output",
        [place, row_weights, act_e, act_s],
        [*down_e, *down_s_t],
        [block_of(length, width - aside), block_of(length, aside)],
        unit * (slots * (length + hidden) + length * padded_s),
    )

    column_parts = lambda values: jnp.split(flat(values), n, axis=1)
    picked, picked_grad, rows_parts, grads_parts = map(
        column_parts, (picked, picked_grad, rows_all, grads_all)
    )
    act_e, act_s, d_gate, d_up, d_shared = map(flat, (act_e, act_s, d_gate, d_up, d_shared))
    grad_gate_e = scatter_dp([lambda p=p: mm("rd,rf->df", p, d_gate) for p in picked], 0)
    grad_up_e = scatter_dp([lambda p=p: mm("rd,rf->df", p, d_up) for p in picked], 0)
    grad_down_e = scatter_dp([lambda p=p: mm("rf,rd->fd", act_e, p) for p in picked_grad], 1)
    grad_s = scatter_dp(
        [
            lambda r=r, g=g: jnp.concatenate(
                [mm("rd,rf->df", r, d_shared), mm("rd,rf->df", g, act_s)], axis=1
            )
            for r, g in zip(rows_parts, grads_parts)
        ],
        0,
    )
    grad_s = grad_s.reshape(groups, rows_w, 3, padded_s)[..., :part_s].astype(bf16)
    d_rows[0] = d_rows[0].astype(f32)
    d_rows, grad_gate_e, grad_up_e, grad_down_e, grad_s, out_parts = lax.optimization_barrier(
        (d_rows, grad_gate_e, grad_up_e, grad_down_e, grad_s, out_parts)
    )
    grad_s = lax.all_to_all(grad_s, "expert", split_axis=0, concat_axis=0, tiled=True)
    grad_s = grad_s.transpose(2, 1, 0, 3).reshape(3, rows_w, hidden_s).astype(f32)
    d_rows_own = turned(jnp.concatenate([d.astype(f32) for d in d_rows], axis=1), dp_count)

    out_grad = cotangent[0].astype(f32)
    middle_part, second_gain_grad = norm_back(d_rows_own, normed_two, scale_two, second_gain)
    middle_grad = out_grad + middle_part
    attn_grad = middle_grad.astype(bf16)
    mixed_grad = mm("rd,dv->rv", attn_grad, output_t).astype(bf16)
    attn_parts = jnp.split(turned(attn_grad, dp_count), n, axis=1)
    early = mixed.shape[1] // 2
    grad_out_t = [lambda p=p: mm("rd,rv->dv", p, mixed[:, :early]) for p in attn_parts]
    if dp_count == 2:
        sent, mixed_grad = lax.optimization_barrier((grad_out_t[1]().astype(bf16), mixed_grad))
        grad_out_t = grad_out_t[0]() + swap(sent).astype(f32)
    else:
        grad_out_t = scatter_dp(grad_out_t, 0)
    grad_out_t = [grad_out_t.astype(bf16), mm("rd,rv->dv", attn_grad, mixed[:, early:]).astype(bf16)]
    out_sum = scatter_rows(after(out_parts[0], d_rows))
    d_nope, d_rope, d_expanded, d_keys_rope = attend_back(
        linear, tables, expanded, rope_keys, bias, mixed_grad, heads
    )
    d_expanded, grad_out_t[0] = lax.optimization_barrier((d_expanded, grad_out_t[0]))
    latent_part = mm("rk,kc->rc", d_expanded, expand_t)
    rope_part = d_keys_rope[:, :ROPE] + d_keys_rope[:, ROPE:]
    latent_rope_part = jnp.concatenate([latent_part, rope_part], axis=-1)
    if dp_count == 2:
        first_half, second_half = latent_rope_part[:length], latent_rope_part[length:]
        is_first = lax.axis_index("dp") == 0
        sent = swap(jnp.where(is_first, second_half, first_half).astype(bf16))
        combined = jnp.where(is_first, first_half, second_half) + sent.astype(f32)
    else:
        combined = lax.psum_scatter(latent_rope_part, "dp", scatter_dimension=0, tiled=True)
    grad_expand_t = mm("rk,rc->kc", d_expanded, latent_all).astype(bf16)
    latent_grad, latent_gain_grad = norm_back(
        combined[:, :RANK], latent_normed, latent_scale, latent_norm
    )
    rope_grad = rotate_back(combined[:, RANK:], cosine, sine)
    linear_grad = jnp.concatenate(
        [d_nope, d_rope, latent_grad.astype(bf16), rope_grad.astype(bf16)], axis=-1
    )
    linear_grad = jnp.pad(linear_grad, ((0, 0), (0, -linear_width % 128)))
    normed_grad = mm("rk,dk->rd", linear_grad, query_latent)
    input_part, first_gain_grad = norm_back(normed_grad, normed_one, scale_one, first_gain)
    tokens_grad = (middle_grad + input_part)[None]
    small = jnp.stack(
        [
            first_gain_grad,
            second_gain_grad,
            jnp.pad(
                latent_gain_grad.reshape(shards, -1), ((0, 0), (0, g1 - RANK // shards))
            ).reshape(-1),
        ],
        axis=1,
    )
    small = jnp.pad(small, ((0, 0), (0, -small.shape[1] % 128))).astype(bf16)
    grad_linear = mm("rd,rk->dk", normed_low, linear_grad).astype(bf16)
    sums = [*grad_out_t, flat(out_parts[1]), grad_expand_t, grad_linear, small]
    over_dp = [False, True, False, True, True, True]
    if dp_count == 2 and groups == 16:
        sums = grad_sums(sums, over_dp)
    else:
        sums = [
            lax.psum_scatter(v, both if o else "expert", scatter_dimension=0, tiled=True)
            for v, o in zip(sums, over_dp)
        ]
        sums = [v.astype(f32) for v in sums]
    *grad_out_t, out_aside, grad_expand_t, grad_linear, small = sums
    out_sum = after(out_sum, grad_linear)
    out_sum = jnp.concatenate([out_sum.astype(f32), out_aside], axis=1)
    outputs = (middle + turned(out_sum, dp_count)).astype(bf16)[None]
    return (
        outputs,
        tokens_grad,
        small[:, 0],
        heads_together(grad_linear[:, :query_width], heads),
        grad_linear[:, query_width:linear_width],
        small[: RANK // shards, 2],
        grad_expand_t.T,
        jnp.concatenate(grad_out_t, axis=1).T,
        small[:, 1],
        grad_s[0],
        grad_s[1],
        grad_s[2].T,
        grad_gate_e[None],
        grad_up_e[None],
        grad_down_e[None],
    )


def solution(mesh):
    rows = P("expert", "dp", None)
    first = P(("dp", "expert"), None)
    last = P(None, ("dp", "expert"))
    vector = P(("dp", "expert"))
    down = P("expert", None, "dp")
    return jax.shard_map(
        local,
        mesh=mesh,
        in_specs=(
            rows,
            P("expert", None),
            rows,
            rows,
            vector,
            first,
            first,
            vector,
            last,
            last,
            vector,
            first,
            first,
            last,
            rows,
            rows,
            down,
            rows,
        ),
        out_specs=(
            rows,
            rows,
            vector,
            first,
            first,
            vector,
            last,
            last,
            vector,
            first,
            first,
            last,
            rows,
            rows,
            down,
        ),
        check_vma=False,
    )
```
